256 devices in a mesh: dom: 64 (over x, z, core), feat: 4 (over y).
Axes of the slice: x: 4, y: 4, z: 8, core: 2. Of those that a mesh axis runs over, the one named last changes fastest.
Arguments:
- features: bfloat16 [65536, 1024], P('dom', 'feat'), may hold values from -6 to 6
- adjacency: bfloat16 [512, 16, 128, 128], P('dom'), may hold values from -0.125 to 0.125
- tile_src: int32 [512, 16], replicated, may hold values from 0 to 511, as said below
- mig_slot: int32 [64, 2], replicated, may hold values from 0 to 7, as said below
- weight_one: bfloat16 [1024, 1024], replicated, may hold values from -0.1875 to 0.1875
- weight_two: bfloat16 [1024, 1024], replicated, may hold values from -0.1875 to 0.1875
Outputs:
- mixed: bfloat16 [65536, 1024], P('dom', 'feat')
The draws below stay inside these ranges and needn't reach their ends.
Inputs may be any that keep to these rules, and one draw needn't show every extreme that they name: `tile_src`: the tiles of the row blocks that one partition holds name at most 2 distinct blocks held by any one other partition, both in the starting placement and in the placement after the move; in the starting placement they name exactly 2 blocks of every other partition, one of which leaves that partition in the move. `mig_slot`: each row holds 2 distinct slots.
All inputs are finite; a program needn't handle non-finite values.
Results may differ from the reference program's by a relative error of at most 0.0064.
Values may be sent and summed in bfloat16 or wider, within the bound.
A program may use at most 128 MiB of HBM per device.

```python
import jax
import jax.numpy as jnp
from jax import lax

F = 1024
B = 128
R = 8
TPB = 16
MIG = 2
NB = 512
NODES = 65536
N_DOM = 64


def pick_list(key, values, usable, filler, wanted, salt):
    block_pool = jnp.concatenate([values, filler], axis=1)
    pool_width = block_pool.shape[1]
    rank_class = jnp.concatenate([jnp.where(usable, 0, 2), jnp.zeros_like(filler) + 1], axis=1).astype(jnp.int32)
    ranking = jnp.argsort(rank_class * pool_width + jnp.arange(pool_width, dtype=jnp.int32)[None, :], axis=1, stable=True)
    chosen = jnp.take_along_axis(block_pool, ranking[:, :wanted], axis=1)
    shuffle_scores = jax.random.randint(jax.random.fold_in(key, salt), (N_DOM, wanted), 0, 1048576) * wanted + jnp.arange(wanted, dtype=jnp.int32)[None, :]
    shuffle = jnp.argsort(shuffle_scores, axis=1, stable=True)
    return jnp.take_along_axis(chosen, shuffle, axis=1)


def layout_draw(key):
    domain_ids = jnp.arange(N_DOM, dtype=jnp.int32)
    slot_scores = jax.random.randint(jax.random.fold_in(key, 11), (N_DOM, R), 0, 1048576) * R + jnp.arange(R, dtype=jnp.int32)[None, :]
    slot_order = jnp.argsort(slot_scores, axis=1, stable=True).astype(jnp.int32)
    mig_slots = slot_order[:, :MIG]
    leave_total = MIG * TPB
    stay_total = (R - MIG) * TPB
    group_count = min(leave_total, N_DOM)
    group_scores = jax.random.randint(jax.random.fold_in(key, 12), (N_DOM,), 0, 1048576) * N_DOM + domain_ids
    group_rank = jnp.argsort(jnp.argsort(group_scores, stable=True), stable=True)
    in_group = group_rank < group_count
    move_pick = jax.random.randint(jax.random.fold_in(key, 13), (N_DOM, N_DOM), 0, MIG)
    stay_pick = jax.random.randint(jax.random.fold_in(key, 14), (N_DOM, N_DOM), 0, R - MIG)
    peer_index = jnp.broadcast_to(domain_ids[None, :], (N_DOM, N_DOM))
    moving_named = peer_index * R + slot_order[peer_index, move_pick]
    staying_named = peer_index * R + slot_order[peer_index, MIG + stay_pick]
    not_self = domain_ids[:, None] != domain_ids[None, :]
    leave_usable = not_self & in_group[None, :]
    stay_usable = not_self & jnp.logical_not(in_group)[None, :]
    own_move = domain_ids[:, None] * R + jnp.take_along_axis(slot_order, jax.random.randint(jax.random.fold_in(key, 15), (N_DOM, leave_total), 0, MIG), axis=1)
    own_stay = domain_ids[:, None] * R + jnp.take_along_axis(slot_order, MIG + jax.random.randint(jax.random.fold_in(key, 16), (N_DOM, stay_total), 0, R - MIG), axis=1)
    leaving_list = pick_list(key, staying_named, leave_usable, own_move, leave_total, 17)
    staying_list = pick_list(key, jnp.concatenate([moving_named, staying_named], axis=1), jnp.concatenate([not_self, stay_usable], axis=1), own_stay, stay_total, 18)
    by_order = jnp.concatenate([leaving_list, staying_list], axis=1).reshape(N_DOM, R, TPB)
    inverse = jnp.argsort(slot_order, axis=1, stable=True)
    listing = jnp.take_along_axis(by_order, inverse[:, :, None], axis=1)
    return (mig_slots.astype(jnp.int32), listing.reshape(N_DOM * R, TPB).astype(jnp.int32))


def draw_tile_src(key, part):
    return layout_draw(key)[1]


def draw_mig_slot(key, part):
    return layout_draw(key)[0]


def levels(rng, dims, pieces, least, high):
    def one(axis_at, parts):
        heights = jax.random.uniform(jax.random.fold_in(jax.random.fold_in(rng, 6), axis_at), (parts,), jnp.float32, least / len(pieces), high / len(pieces))
        return jnp.repeat(jnp.exp(heights), dims[axis_at] // parts).reshape((-1,) + (1,) * (len(dims) - axis_at - 1))

    factor_of = one(*pieces[0])
    for cut in pieces[1:]:
        factor_of = factor_of * one(*cut)
    return factor_of


def noise(stream_key, extent, width, most, cuts=(), held_as=jnp.bfloat16):
    values = width * jax.random.normal(stream_key, extent, jnp.float32)
    if cuts:
        values = values * levels(stream_key, extent, cuts, -0.22, 0.18)
    return jnp.clip(values, -most, most).astype(held_as)


def setup_inputs(seed: int = 0) -> dict:
    streams_of = jax.random.split(jax.random.key(seed), 7)
    features = noise(streams_of[0], (NODES, F), 1.0, 6.0, ((0, 64), (1, 4)))
    adjacency = noise(streams_of[1], (NB, TPB, B, B), (TPB * B) ** -0.5, 0.125, ((0, 64),))
    tile_src = draw_tile_src(jax.random.fold_in(streams_of[6], 71), 0)
    mig_slot = draw_mig_slot(jax.random.fold_in(streams_of[6], 71), 0)
    weight_one = noise(streams_of[4], (F, F), F ** -0.5, 0.1875)
    weight_two = noise(streams_of[5], (F, F), F ** -0.5, 0.1875)
    return {"features": features, "adjacency": adjacency, "tile_src": tile_src, "mig_slot": mig_slot, "weight_one": weight_one, "weight_two": weight_two}


def apply_layer(inputs, adjacency, tile_src, weight):
    def per_domain(domain):
        source_ids = lax.dynamic_slice_in_dim(tile_src, domain * R, R, 0)
        tiles_here = lax.dynamic_slice_in_dim(adjacency, domain * R, R, 0)
        gathered = inputs[source_ids]
        summed = jnp.einsum('rtij,rtjf->rif', tiles_here.astype(jnp.float32), gathered.astype(jnp.float32))
        agg_rows = summed.astype(jnp.bfloat16).reshape(R * B, F)
        return jnp.dot(agg_rows, weight, preferred_element_type=jnp.float32)
    result = lax.map(per_domain, jnp.arange(N_DOM, dtype=jnp.int32))
    return result.reshape(N_DOM * R, B, F)


def reference(features, adjacency, tile_src, mig_slot, weight_one, weight_two):
    blocks_in = features.reshape(N_DOM * R, B, F)
    hidden = jax.nn.relu(apply_layer(blocks_in, adjacency, tile_src, weight_one)).astype(jnp.bfloat16)
    result = apply_layer(hidden, adjacency, tile_src, weight_two)
    domain_ids = jnp.arange(N_DOM, dtype=jnp.int32)
    block_ids = (domain_ids[:, None] * R + jnp.arange(R, dtype=jnp.int32)[None, :]).astype(jnp.int32)
    previous = (((domain_ids - 1) % N_DOM) * R)[:, None] + jnp.roll(mig_slot, 1, axis=0)
    new_ids = block_ids.at[domain_ids[:, None], mig_slot].set(previous.astype(jnp.int32))
    placed = result[new_ids.reshape(-1)]
    return placed.reshape(N_DOM * R * B, F).astype(jnp.bfloat16)
```

```python
import functools

import jax
import jax.numpy as jnp
from jax import lax
from jax.experimental import pallas as pl
from jax.experimental.pallas import tpu as pltpu
from jax.sharding import PartitionSpec as P

B = 128
R = 8
TPB = 16
NX, NZ, NC, NY = 4, 8, 2, 4
COLS = 256
ROWS = R * B
TILES = R * TPB
CAP = 34
LIST = 48
MESH = pl.DeviceIdType.MESH
BF, F32 = jnp.bfloat16, jnp.float32
VMEM_LIMIT = 60 * 1024 * 1024


class Place:
    def __init__(self):
        d = lax.axis_index("dom")
        self.dom = d
        self.y = lax.axis_index("feat")
        self.x = d // (NZ * NC)
        self.z = lax.rem(d // NC, NZ)
        self.c = lax.rem(d, NC)

    def at(self, dx=0, dz=0, sibling=False, dy=0):
        x = lax.rem(self.x + (dx + NX), NX)
        z = lax.rem(self.z + (dz + NZ), NZ)
        c = 1 - self.c if sibling else self.c
        y = lax.rem(self.y + (dy + NY), NY)
        return ((x * NZ + z) * NC + c, y)

    def ring(self, by):
        return (lax.rem(self.dom + (by + NX * NZ * NC), NX * NZ * NC), self.y)


def meet(partners, come_from):
    barrier = pltpu.get_barrier_semaphore()
    for p in partners:
        pl.semaphore_signal(barrier, inc=1, device_id=p, device_id_type=MESH)
    pl.semaphore_wait(barrier, come_from)


def remote(src, dst, send, recv, device):
    return pltpu.make_async_remote_copy(
        src_ref=src, dst_ref=dst, send_sem=send, recv_sem=recv, device_id=device, device_id_type=MESH
    )


def pack_kernel(src_ref, adj_ref, send_ref, own_ref, list_ref, start_ref, adj, sem):
    x = lax.axis_index("dom") // (NZ * NC)
    y = lax.axis_index("feat")
    load = pltpu.make_async_copy(adj_ref, adj, sem)
    load.start()
    send_ref[...] = jnp.zeros_like(send_ref)
    own_ref[...] = jnp.zeros_like(own_ref)

    def row(r, counts):
        for p in range(NX):
            start_ref[p * 16 + r] = counts[p]

        def tile(j, counts):
            t = r * TPB + j
            new = []
            for p in range(NX):
                s = src_ref[p * TILES + t]
                list_ref[p * LIST + counts[p]] = t * TILES + lax.rem(s, 128)
                new.append(counts[p] + jnp.where(s // 128 == x, 1, 0))
            return tuple(new)

        return lax.fori_loop(0, TPB, tile, counts, unroll=4)

    zero = jnp.int32(0)
    counts = lax.fori_loop(0, R, row, (zero,) * NX)
    for p in range(NX):
        start_ref[p * 16 + R] = counts[p]
    load.wait()
    lo = pl.multiple_of(y * 32, 32)

    def pack(t, taken):
        col = src_ref[x * TILES + t] // 128
        shift = col * 8
        at = jnp.bitwise_and(lax.shift_right_logical(taken, shift), 255)
        send_ref[col, at] = adj[t, pl.ds(lo, 32), :]
        return taken + lax.shift_left(jnp.int32(1), shift)

    lax.fori_loop(0, TILES, pack, zero, unroll=4)

    def keep(j, _):
        t = list_ref[x * LIST + j] // TILES
        own_ref[j] = adj[t]
        return 0

    lax.fori_loop(0, counts_at(start_ref, x), keep, 0)


def counts_at(start_ref, x):
    return start_ref[x * 16 + R]


def pack(sources, adjacency):
    smem = pl.BlockSpec(memory_space=pltpu.SMEM)
    vmem = pl.BlockSpec(memory_space=pltpu.VMEM)
    return pl.pallas_call(
        pack_kernel,
        name="pack_tiles",
        out_shape=(
            jax.ShapeDtypeStruct((NX, CAP, 32, B), BF),
            jax.ShapeDtypeStruct((CAP, B, B), BF),
            jax.ShapeDtypeStruct((NX * LIST,), jnp.int32),
            jax.ShapeDtypeStruct((NX * 16,), jnp.int32),
        ),
        in_specs=[smem, pl.BlockSpec(memory_space=pl.ANY)],
        out_specs=(vmem, vmem, smem, smem),
        scratch_shapes=[pltpu.VMEM((TILES, B, B), BF), pltpu.SemaphoreType.DMA],
        compiler_params=pltpu.CompilerParams(vmem_limit_bytes=VMEM_LIMIT),
    )(sources, adjacency.reshape(TILES, B, B))


class Ring:
    def __init__(self, me, np_, own, gathered, sems):
        self.me, self.np, self.own, self.gathered = me, np_, own, gathered
        self.zs, self.zr, self.ss, self.sr = sems
        self.per = R // np_
        self.started = []

    @staticmethod
    def scratch(np_):
        n = 2 * 4 * np_
        return [
            pltpu.SemaphoreType.DMA((n,)),
            pltpu.SemaphoreType.DMA((n,)),
            pltpu.SemaphoreType.DMA((NZ * np_,)),
            pltpu.SemaphoreType.DMA((NZ * np_,)),
        ]

    def has(self, way, s, k):
        if s < 3:
            return True
        return s == 3 and (k < self.np // 2) == (way == 0)

    def spot(self, hops, sibling, k):
        zo = lax.rem(self.me.z + (NZ - hops), NZ)
        c = 1 - self.me.c if sibling else self.me.c
        return self.gathered.at[zo, c, pl.ds(k * self.per, self.per)]

    def z_copy(self, way, s, k):
        hops = s if way == 0 else -s
        i = (way * 4 + s) * self.np + k
        src = self.own(k) if s == 0 else self.spot(hops, False, k)
        return remote(
            src,
            self.spot(hops, False, k),
            self.zs.at[i],
            self.zr.at[i],
            self.me.at(dz=1 if way == 0 else -1),
        )

    def z_arrival(self, way, s, k):
        hops = s + 1 if way == 0 else -(s + 1)
        i = (way * 4 + s) * self.np + k
        spot = self.spot(hops, False, k)
        return remote(spot, spot, self.zs.at[i], self.zr.at[i], self.me.at(dz=-1 if way == 0 else 1))

    def rel(self, hops):
        return (hops + NZ) % NZ

    def sib_copy(self, hops, k):
        i = self.rel(hops) * self.np + k
        src = self.own(k) if hops == 0 else self.spot(hops, False, k)
        return remote(src, self.spot(hops, False, k), self.ss.at[i], self.sr.at[i], self.me.at(sibling=True))

    def sib_arrival(self, hops, k):
        i = self.rel(hops) * self.np + k
        spot = self.spot(hops, True, k)
        return remote(spot, spot, self.ss.at[i], self.sr.at[i], self.me.at(sibling=True))

    def start(self, copy):
        copy.start()
        self.started.append(copy)

    def send_own(self, k):
        for way in range(2):
            self.start(self.z_copy(way, 0, k))
        self.start(self.sib_copy(0, k))

    def arrive(self, s, k):
        for way in range(2):
            if not self.has(way, s, k):
                continue
            self.z_arrival(way, s, k).wait_recv()
            if self.has(way, s + 1, k):
                self.start(self.z_copy(way, s + 1, k))
            self.start(self.sib_copy(s + 1 if way == 0 else -(s + 1), k))

    def finish(self):
        for rel in range(NZ):
            for k in range(self.np):
                self.sib_arrival(rel, k).wait_recv()
        for copy in self.started:
            copy.wait_send()


def first_kernel(x_ref, send_ref, own_ref, gath_ref, tiles_ref, zs, zr, ss, sr, xs, xr, ys, yr, loc):
    me = Place()
    partners = [me.at(dz=1), me.at(dz=-1), me.at(sibling=True), me.at(dy=1), me.at(dy=-1)]
    partners += [me.at(dx=1), me.at(dx=-1), me.at(dx=2)]
    meet(partners, len(partners))

    np_ = 2
    ring = Ring(me, np_, lambda k: x_ref.at[pl.ds(k * (R // np_), R // np_)], gath_ref, (zs, zr, ss, sr))
    keep_x = pltpu.make_async_copy(x_ref, gath_ref.at[me.z, me.c], loc.at[0])
    keep_t = pltpu.make_async_copy(own_ref, tiles_ref.at[me.x], loc.at[1])
    for k in range(np_):
        ring.send_own(k)

    half = CAP // 2
    started = []

    def go(copy):
        copy.start()
        started.append(copy)

    def quarter(dx, dy, lo=0, n=CAP):
        x = lax.rem(me.x + (dx + NX), NX)
        y = lax.rem(me.y + (dy + NY), NY)
        return tiles_ref.at[x, pl.ds(lo, n), pl.ds(pl.multiple_of(y * 32, 32), 32), :]

    for i, dx in enumerate((1, -1, 2)):
        x_to = lax.rem(me.x + (dx + NX), NX)
        go(remote(send_ref.at[x_to], quarter(0, 0), xs.at[i], xr.at[i], me.at(dx=dx)))
    keep_x.start()
    keep_t.start()

    froms = (-1, 1, 2)

    def tiles_from_x(i):
        spot = quarter(froms[i], 0)
        remote(spot, spot, xs.at[i], xr.at[i], me.at(dx=froms[i])).wait_recv()
        go(remote(spot, spot, ys.at[i * 4], yr.at[i * 4], me.at(dy=1)))
        go(remote(spot, spot, ys.at[i * 4 + 1], yr.at[i * 4 + 1], me.at(dy=-1)))

    def tiles_from_y(i):
        for way, dy in ((0, -1), (1, 1)):
            spot = quarter(froms[i], dy)
            sem = i * 4 + way
            remote(spot, spot, ys.at[sem], yr.at[sem], me.at(dy=dy)).wait_recv()
            part = quarter(froms[i], dy, way * half, half)
            go(remote(part, part, ys.at[sem + 2], yr.at[sem + 2], me.at(dy=-dy)))

    def tiles_last(i):
        for way, dy in ((0, -1), (1, 1)):
            spot = quarter(froms[i], 2, way * half, half)
            sem = i * 4 + way + 2
            remote(spot, spot, ys.at[sem], yr.at[sem], me.at(dy=dy)).wait_recv()

    ring.arrive(0, 0)
    tiles_from_x(0)
    tiles_from_x(1)
    ring.arrive(0, 1)
    ring.arrive(1, 0)
    tiles_from_x(2)
    tiles_from_y(0)
    ring.arrive(1, 1)
    tiles_from_y(1)
    ring.arrive(2, 0)
    tiles_from_y(2)
    ring.arrive(2, 1)
    ring.arrive(3, 0)
    ring.arrive(3, 1)
    for i in range(3):
        tiles_last(i)
    ring.finish()
    for copy in started:
        copy.wait_send()
    keep_x.wait()
    keep_t.wait()


def first_exchange(blocks, send, own):
    hbm = pl.BlockSpec(memory_space=pl.ANY)
    return pl.pallas_call(
        first_kernel,
        name="exchange_tiles_and_features",
        out_shape=(
            jax.ShapeDtypeStruct((NZ, NC, R, B, COLS), BF),
            jax.ShapeDtypeStruct((NX, CAP, B, B), BF),
        ),
        in_specs=[hbm, hbm, hbm],
        out_specs=(hbm, hbm),
        scratch_shapes=[
            *Ring.scratch(2),
            pltpu.SemaphoreType.DMA((3,)),
            pltpu.SemaphoreType.DMA((3,)),
            pltpu.SemaphoreType.DMA((12,)),
            pltpu.SemaphoreType.DMA((12,)),
            pltpu.SemaphoreType.DMA((2,)),
        ],
        compiler_params=pltpu.CompilerParams(collective_id=0, has_side_effects=True),
    )(blocks, send, own)


def partial_kernel(list_ref, start_ref, tiles_ref, gath_ref, part_ref, own_ref, prod):
    p = pl.program_id(0)

    def one(j, _):
        s = jnp.bitwise_and(list_ref[p * LIST + j], 127)
        prod[j] = jnp.dot(tiles_ref[0, j], gath_ref[s], preferred_element_type=F32)
        return 0

    count = start_ref[p * 16 + R]
    lax.fori_loop(0, (count + 1) // 2, lambda i, _: one(2 * i + 1, one(2 * i, 0)), 0)
    mine = p == lax.axis_index("dom") // (NZ * NC)

    def row(r, _):
        total = lax.fori_loop(
            start_ref[p * 16 + r],
            start_ref[p * 16 + r + 1],
            lambda j, acc: acc + prod[j],
            jnp.zeros((B, COLS), F32),
        )
        at = pl.ds(pl.multiple_of(r * B, B), B)
        part_ref[0, at] = total.astype(BF)

        @pl.when(mine)
        def _():
            own_ref[at] = total

        return 0

    lax.fori_loop(0, R, row, 0)


def partial_sums(lists, starts, tiles, gathered):
    smem = pl.BlockSpec(memory_space=pltpu.SMEM)
    return pl.pallas_call(
        partial_kernel,
        name="partial_aggregate",
        grid=(NX,),
        out_shape=(
            jax.ShapeDtypeStruct((NX, ROWS, COLS), BF),
            jax.ShapeDtypeStruct((ROWS, COLS), F32),
        ),
        in_specs=[
            smem,
            smem,
            pl.BlockSpec((1, CAP, B, B), lambda p: (p, 0, 0, 0)),
            pl.BlockSpec((NZ * NC * R, B, COLS), lambda p: (0, 0, 0)),
        ],
        out_specs=(
            pl.BlockSpec((1, ROWS, COLS), lambda p: (p, 0, 0)),
            pl.BlockSpec((ROWS, COLS), lambda p: (0, 0)),
        ),
        scratch_shapes=[pltpu.VMEM((CAP, B, COLS), F32)],
        compiler_params=pltpu.CompilerParams(vmem_limit_bytes=VMEM_LIMIT),
    )(lists, starts, tiles, gathered.reshape(NZ * NC * R, B, COLS))


NCH = 4
RC = ROWS // NCH
HC = RC // 2


def finish_kernel(last, *refs):
    if last:
        part, own, weight, slots, where, out = refs[:6]
        refs = refs[6:]
    else:
        part, own, weight, gath_ref = refs[:4]
        refs = refs[4:]
    relay_in, relay_out, sums_in, agg, done, xs, xr, ys, yr = refs[:9]
    refs = refs[9:]
    me = Place()
    partners = [me.at(dx=1), me.at(dx=-1), me.at(dy=1), me.at(dy=-1)]
    if last:
        leave, came, ms, mr = refs
        partners += [me.ring(1), me.ring(-1)]
    else:
        loc = refs[4]
        partners += [me.at(dz=1), me.at(dz=-1), me.at(sibling=True)]
        ring = Ring(me, NCH, lambda k: done.at[pl.ds(k * (R // NCH), R // NCH)], gath_ref, refs[:4])
    meet(partners, len(partners))

    started = []

    def go(copy):
        copy.start()
        started.append(copy)

    ways = ((0, 1), (1, -1))
    side = lambda dx: lax.rem(me.x + (dx + NX), NX)
    halves = lambda k: (pl.ds(k * RC, HC), pl.ds(k * RC + HC, HC))

    def x_far(k):
        for way, d in ways:
            i = (way * NCH + k) * 3
            go(remote(part.at[side(2), halves(k)[way]], relay_in.at[way, k], xs.at[i], xr.at[i], me.at(dx=d)))

    def x_near(k):
        for way, d in ways:
            i = (way * NCH + k) * 3 + 1
            rows = halves(k)[1 - way]
            go(remote(part.at[side(d), rows], sums_in.at[way, rows], xs.at[i], xr.at[i], me.at(dx=d)))

    def x_relay(k):
        for way, d in ways:
            i = (way * NCH + k) * 3
            spot = relay_in.at[way, k]
            remote(spot, spot, xs.at[i], xr.at[i], me.at(dx=-d)).wait_recv()
            rows = halves(k)[way]
            mine = part[side(d), rows, :].astype(F32)
            relay_out[way, k] = (mine + relay_in[way, k].astype(F32)).astype(BF)
            go(remote(relay_out.at[way, k], sums_in.at[way, rows], xs.at[i + 2], xr.at[i + 2], me.at(dx=d)))

    def x_sum(k):
        for way, d in ways:
            for j, rows in ((1, halves(k)[1 - way]), (2, halves(k)[way])):
                i = (way * NCH + k) * 3 + j
                spot = sums_in.at[way, rows]
                remote(spot, spot, xs.at[i], xr.at[i], me.at(dx=-d)).wait_recv()
        rows = pl.ds(k * RC, RC)
        total = own[rows, :] + sums_in[0, rows, :].astype(F32) + sums_in[1, rows, :].astype(F32)
        agg[me.y, rows, :] = total.astype(BF)
        for way, d in ways:
            i = (way * NCH + k) * 2
            spot = agg.at[me.y, rows]
            go(remote(spot, spot, ys.at[i], yr.at[i], me.at(dy=d)))

    def y_pass(k):
        for way, d in ways:
            i = (way * NCH + k) * 2
            y_from = lax.rem(me.y + (NY - d), NY)
            spot = agg.at[y_from, pl.ds(k * RC, RC)]
            remote(spot, spot, ys.at[i], yr.at[i], me.at(dy=-d)).wait_recv()
            spot = agg.at[y_from, halves(k)[way]]
            go(remote(spot, spot, ys.at[i + 1], yr.at[i + 1], me.at(dy=d)))

    def transform(k):
        for way, d in ways:
            i = (way * NCH + k) * 2 + 1
            spot = agg.at[lax.rem(me.y + 2, NY), halves(k)[way]]
            remote(spot, spot, ys.at[i], yr.at[i], me.at(dy=-d)).wait_recv()
        rows = pl.ds(k * RC, RC)
        total = jnp.zeros((RC, COLS), F32)
        for y in range(NY):
            total += jnp.dot(agg[y, rows, :], weight[pl.ds(y * COLS, COLS), :], preferred_element_type=F32)
        if not last:
            total = jnp.maximum(total, 0.0)
        done[pl.ds(k * (R // NCH), R // NCH)] = total.astype(BF).reshape(R // NCH, B, COLS)
        if not last:
            ring.send_own(k)
            copy = pltpu.make_async_copy(
                done.at[pl.ds(k * (R // NCH), R // NCH)],
                gath_ref.at[me.z, me.c, pl.ds(k * (R // NCH), R // NCH)],
                loc.at[k],
            )
            copy.start()
            kept.append(copy)

    kept = []
    x_far(0)
    for slot in range(NCH + 3):
        if slot + 1 < NCH:
            x_far(slot + 1)
        if slot < NCH:
            x_near(slot)
            x_relay(slot)
        if 0 <= slot - 1 < NCH:
            x_sum(slot - 1)
        if 0 <= slot - 2 < NCH:
            y_pass(slot - 2)
        if 0 <= slot - 3 < NCH:
            transform(slot - 3)
        if not last:
            for s in range(4):
                k = slot - 4 - s
                if 0 <= k < NCH:
                    ring.arrive(s, k)
    if last:
        for m in range(2):
            leave[m] = done[slots[m]]
        move = remote(leave, came, ms, mr, me.ring(1))
        move.start()
        move.wait()
        done[pl.ds(R, 2)] = came[...]
        for r in range(R):
            out[pl.ds(r * B, B), :] = done[where[r]]
    else:
        for slot in range(NCH + 3, NCH + 3 + 8):
            for s in range(4):
                k = slot - 4 - s
                if 0 <= k < NCH:
                    ring.arrive(s, k)
        ring.finish()
        for copy in kept:
            copy.wait()
    for copy in started:
        copy.wait_send()


def finish(last, part, own, weight, slots=None, where=None):
    vmem = pl.BlockSpec(memory_space=pltpu.VMEM)
    smem = pl.BlockSpec(memory_space=pltpu.SMEM)
    scratch = [
        pltpu.VMEM((2, NCH, HC, COLS), BF),
        pltpu.VMEM((2, NCH, HC, COLS), BF),
        pltpu.VMEM((2, ROWS, COLS), BF),
        pltpu.VMEM((NY, ROWS, COLS), BF),
        pltpu.VMEM((R + 2, B, COLS), BF),
        pltpu.SemaphoreType.DMA((2 * NCH * 3,)),
        pltpu.SemaphoreType.DMA((2 * NCH * 3,)),
        pltpu.SemaphoreType.DMA((2 * NCH * 2,)),
        pltpu.SemaphoreType.DMA((2 * NCH * 2,)),
    ]
    if last:
        scratch += [pltpu.VMEM((2, B, COLS), BF), pltpu.VMEM((2, B, COLS), BF), pltpu.SemaphoreType.DMA, pltpu.SemaphoreType.DMA]
        out_shape = jax.ShapeDtypeStruct((ROWS, COLS), BF)
        out_spec = vmem
        args, in_specs = (part, own, weight, slots, where), [vmem, vmem, vmem, smem, smem]
    else:
        scratch += [*Ring.scratch(NCH), pltpu.SemaphoreType.DMA((NCH,))]
        out_shape = jax.ShapeDtypeStruct((NZ, NC, R, B, COLS), BF)
        out_spec = pl.BlockSpec(memory_space=pl.ANY)
        args, in_specs = (part, own, weight), [vmem, vmem, vmem]
    return pl.pallas_call(
        functools.partial(finish_kernel, last),
        name="layer_two_end" if last else "layer_one_end",
        out_shape=out_shape,
        in_specs=in_specs,
        out_specs=out_spec,
        scratch_shapes=scratch,
        compiler_params=pltpu.CompilerParams(
            collective_id=2 if last else 1, has_side_effects=True, vmem_limit_bytes=VMEM_LIMIT
        ),
    )(*args)


def on_device(features, adjacency, tile_src, mig_slot, weight_one, weight_two):
    dom = lax.axis_index("dom")
    z, c = lax.rem(dom // NC, NZ), lax.rem(dom, NC)
    grid = tile_src.reshape(NX, NZ, NC, TILES)
    sources = lax.dynamic_slice(grid, (0, z, c, 0), (NX, 1, 1, TILES)).reshape(NX * TILES)
    slots = lax.dynamic_slice_in_dim(mig_slot, dom, 1, 0).reshape(2)
    spot = jnp.arange(R, dtype=jnp.int32)
    where = jnp.where(spot == slots[0], R, jnp.where(spot == slots[1], R + 1, spot))
    col = lax.axis_index("feat") * COLS
    w_one = lax.dynamic_slice_in_dim(weight_one, col, COLS, 1)
    w_two = lax.dynamic_slice_in_dim(weight_two, col, COLS, 1)

    send, own, lists, starts = pack(sources, adjacency)
    gathered, tiles = first_exchange(features.reshape(R, B, COLS), send, own)
    part, mine = partial_sums(lists, starts, tiles, gathered)
    gathered = finish(False, part, mine, w_one)
    part, mine = partial_sums(lists, starts, tiles, gathered)
    return finish(True, part, mine, w_two, slots, where)


def solution(mesh):
    in_specs = (P("dom", "feat"), P("dom", None, None, None), P(), P(), P(), P())
    return jax.shard_map(
        on_device, mesh=mesh, in_specs=in_specs, out_specs=P("dom", "feat"), check_vma=False
    )
```

```python
import functools

import jax
import jax.numpy as jnp
from jax import lax
from jax.experimental import pallas as pl
from jax.experimental.pallas import tpu as pltpu
from jax.sharding import PartitionSpec as P

B = 128
R = 8
TPB = 16
NX, NZ, NC, NY = 4, 8, 2, 4
NDOM = NX * NZ * NC
COLS = 256
ROWS = R * B
TILES = R * TPB
PAIRS = NZ * NC + 1
SLOTS = 2 * PAIRS
QROWS = B // NY
NP = 4
RC = ROWS // NP
HC = RC // 2
PER = R // NP
MESH = pl.DeviceIdType.MESH
BF, F32 = jnp.bfloat16, jnp.float32
WAYS = ((0, 1), (1, -1))


class Place:
    def __init__(self):
        d = lax.axis_index("dom")
        self.dom = d
        self.y = lax.axis_index("feat")
        self.x = d // (NZ * NC)
        self.z = lax.rem(d // NC, NZ)
        self.c = lax.rem(d, NC)

    def at(self, dx=0, dz=0, sibling=False, dy=0):
        x = lax.rem(self.x + (dx + NX), NX)
        z = lax.rem(self.z + (dz + NZ), NZ)
        c = 1 - self.c if sibling else self.c
        y = lax.rem(self.y + (dy + NY), NY)
        return ((x * NZ + z) * NC + c, y)

    def along(self, by):
        return (lax.rem(self.dom + (by + NDOM), NDOM), self.y)

    def y_of(self, dy):
        return lax.rem(self.y + (dy + NY), NY)


def remote(src, dst, send, recv, device):
    return pltpu.make_async_remote_copy(
        src_ref=src, dst_ref=dst, send_sem=send, recv_sem=recv, device_id=device, device_id_type=MESH
    )


def table_kernel(src_ref, tab_ref):
    x = lax.axis_index("dom") // (NZ * NC)
    t_row = lax.broadcasted_iota(jnp.int32, (1, TILES), 1)
    earlier = lax.broadcasted_iota(jnp.int32, (TILES, TILES), 0) < lax.broadcasted_iota(jnp.int32, (TILES, TILES), 1)
    lane = lax.broadcasted_iota(jnp.int32, (40, 128), 1)
    slot = lax.broadcasted_iota(jnp.int32, (40, TILES), 0)
    total = jnp.zeros((40, 128), F32)

    def ranks(i):
        s = src_ref[pl.ds(lax.rem(x + i, NX), 1), :]
        q = lax.shift_right_logical(s, 3)
        down = jnp.transpose(jnp.broadcast_to(q, (TILES, TILES)))
        same = jnp.where(jnp.logical_and(down == q, earlier), 1.0, 0.0)
        return s, q, jnp.sum(same, axis=0, keepdims=True)

    def column(total, at, s, q, rank, col):
        here = lax.shift_right_logical(q, 4) == col
        regular = jnp.logical_and(here, rank < 1.5)
        more = jnp.logical_and(here, rank > 1.5)
        first = jnp.min(jnp.where(more, t_row, TILES), axis=1, keepdims=True)
        place = jnp.where(
            regular,
            2 * jnp.bitwise_and(q, 15) + rank.astype(jnp.int32),
            jnp.where(more, SLOTS - 2 + jnp.where(t_row > first, 1, 0), -1),
        )
        entry = (1 + t_row * 128 + jnp.bitwise_and(s, 127)).astype(F32)
        found = jnp.sum(jnp.where(slot == place, entry, 0.0), axis=1, keepdims=True)
        return total + jnp.where(lane == at, found, 0.0)

    own = ranks(0)
    for i in range(NX):
        total = column(total, i, *(own if i == 0 else ranks(i)), x)
        total = column(total, NX + i, *own, lax.rem(x + i, NX))
    tab_ref[...] = total.astype(jnp.int32)


def tables(sources):
    vmem = pl.BlockSpec(memory_space=pltpu.VMEM)
    return pl.pallas_call(
        table_kernel,
        name="tile_tables",
        out_shape=jax.ShapeDtypeStruct((40, 128), jnp.int32),
        in_specs=[vmem],
        out_specs=vmem,
    )(sources)


def ring_scratch():
    n = 2 * 4 * NP
    return [pltpu.SemaphoreType.DMA((n,)), pltpu.SemaphoreType.DMA((n,))] + [
        pltpu.SemaphoreType.DMA((NZ * NP,)),
        pltpu.SemaphoreType.DMA((NZ * NP,)),
    ]


def end_scratch():
    return [
        pltpu.VMEM((NX, ROWS, COLS), BF),
        pltpu.VMEM((2, NP, HC, COLS), BF),
        pltpu.VMEM((2, NP, HC, COLS), BF),
        pltpu.VMEM((2, ROWS, COLS), BF),
        pltpu.VMEM((NY, ROWS, COLS), BF),
        pltpu.SemaphoreType.DMA((2 * NP * 3,)),
        pltpu.SemaphoreType.DMA((2 * NP * 3,)),
        pltpu.SemaphoreType.DMA((2 * NP * 2,)),
        pltpu.SemaphoreType.DMA((2 * NP * 2,)),
    ]


class Ring:
    def __init__(self, me, blocks, own, sems):
        self.me, self.blocks, self.own = me, blocks, own
        self.zs, self.zr, self.ss, self.sr = sems

    def spot(self, hops, side, k):
        return self.blocks[hops % NZ][side].at[pl.ds(k * PER, PER)]

    def source(self, hops, k):
        return self.own(k) if hops % NZ == 0 else self.spot(hops, 0, k)

    def z_copy(self, way, s, k):
        hops = s if way == 0 else -s
        on = s + 1 if way == 0 else -(s + 1)
        i = (way * 4 + s) * NP + k
        up = 1 if way == 0 else -1
        return remote(self.source(hops, k), self.spot(on, 0, k), self.zs.at[i], self.zr.at[i], self.me.at(dz=up))

    def z_arrival(self, way, s, k):
        spot = self.spot(s + 1 if way == 0 else -(s + 1), 0, k)
        i = (way * 4 + s) * NP + k
        return remote(spot, spot, self.zs.at[i], self.zr.at[i], self.me.at(dz=-1 if way == 0 else 1))

    def sib_copy(self, hops, k):
        i = (hops % NZ) * NP + k
        return remote(
            self.source(hops, k), self.spot(hops, 1, k), self.ss.at[i], self.sr.at[i], self.me.at(sibling=True)
        )

    def sib_arrival(self, hops, k):
        i = (hops % NZ) * NP + k
        spot = self.spot(hops, 1, k)
        return remote(spot, spot, self.ss.at[i], self.sr.at[i], self.me.at(sibling=True))

    def send_own(self, k):
        for way in range(2):
            self.z_copy(way, 0, k).start()
        self.sib_copy(0, k).start()

    def arrive(self, way, s, k, on):
        self.z_arrival(way, s, k).wait_recv()
        if on:
            self.z_copy(way, s + 1, k).start()
        self.sib_copy(s + 1 if way == 0 else -(s + 1), k).start()

    def from_sibling(self, *hops):
        for h in hops:
            for k in range(NP):
                self.sib_arrival(h, k).wait_recv()

    def finish(self):
        for way in range(2):
            for s in range(4):
                for k in range(NP):
                    if s < 3 or (k < NP // 2) == (way == 0):
                        self.z_copy(way, s, k).wait_send()
        for h in range(NZ):
            for k in range(NP):
                self.sib_copy(h, k).wait_send()

    def run(self, between):
        for s in range(4):
            if s:
                self.from_sibling(*sorted({(s - 1) % NZ, -(s - 1) % NZ}))

            def turn(k, _, ways=(0, 1), s=s):
                for way in ways:
                    self.arrive(way, s, k, s < 2)
                if s:
                    between(s - 1, k)
                return 0

            if s < 2:
                lax.fori_loop(0, NP, turn, 0)
            elif s == 2:

                def third(k, _, way=0):
                    for w in range(2):
                        self.arrive(w, 2, k, w == way)
                    between(1, k)
                    return 0

                lax.fori_loop(0, NP // 2, third, 0)
                lax.fori_loop(NP // 2, NP, functools.partial(third, way=1), 0)
            else:
                lax.fori_loop(0, NP // 2, functools.partial(turn, ways=(0,)), 0)
                lax.fori_loop(NP // 2, NP, functools.partial(turn, ways=(1,)), 0)
        self.from_sibling(3, -3 % NZ)
        self.from_sibling(4)


STEPS = (
    ((0, 0), (0, 1)),
    ((1, 0), (1, 1), (7, 0), (7, 1)),
    ((2, 0), (2, 1), (6, 0), (6, 1)),
    ((3, 0), (3, 1), (5, 0), (5, 1)),
    ((4, 0), (4, 1)),
)


def whole_kernel(tab, mig, x_ref, adj_ref, w1_ref, w2_ref, out, *refs):
    refs = list(refs)

    def take(n):
        head = refs[:n]
        del refs[:n]
        return head

    flat = [take(2 * NZ) for _ in range(2)]
    blocks = [[f[2 * h : 2 * h + 2] for h in range(NZ)] for f in flat]
    adj, tiles, send, w1, w2, acc, lhs, rhs, done, leave, came = take(11)
    loc, xs, xr, ys, yr, ms, mr = take(7)
    ring_sems = [take(4) for _ in range(2)]
    ends = [take(9) for _ in range(2)]
    me = Place()

    col = pl.ds(pl.multiple_of(me.y * COLS, COLS), COLS)
    loads = [
        pltpu.make_async_copy(adj_ref, adj, loc.at[0]),
        pltpu.make_async_copy(x_ref, blocks[0][0][0], loc.at[1]),
        pltpu.make_async_copy(w1_ref.at[:, col], w1, loc.at[2]),
        pltpu.make_async_copy(w2_ref.at[:, col], w2, loc.at[3]),
    ]
    for load in loads:
        load.start()

    partners = [me.at(dz=1), me.at(dz=-1), me.at(sibling=True), me.at(dy=1), me.at(dy=-1)]
    partners += [me.at(dx=1), me.at(dx=-1), me.at(dx=2), me.along(1), me.along(-1)]
    barrier = pltpu.get_barrier_semaphore()
    for p in partners:
        pl.semaphore_signal(barrier, inc=1, device_id=p, device_id_type=MESH)
    pl.semaphore_wait(barrier, len(partners))

    rings = [
        Ring(me, blocks[0], lambda k: x_ref.at[pl.ds(k * PER, PER)], ring_sems[0]),
        Ring(me, blocks[1], lambda k: blocks[1][0][0].at[pl.ds(k * PER, PER)], ring_sems[1]),
    ]
    for k in range(NP):
        rings[0].send_own(k)

    started = []

    def go(copy):
        copy.start()
        started.append(copy)

    q_rows = lambda dy: pl.ds(pl.multiple_of(me.y_of(dy) * QROWS, QROWS), QROWS)
    loads[0].wait()

    def found(j, column):
        entry = tab[j, column]
        return entry, lax.shift_right_logical(jnp.maximum(entry - 1, 0), 7)

    def pack(i, dx, j, _):
        for k in range(2):
            entry, t = found(2 * j + k, NX + dx % NX)
            part = adj[t, q_rows(0), :]
            send[i, j, :, k * B : (k + 1) * B] = jnp.where(entry > 0, part, jnp.zeros_like(part))
        return 0

    def keep(j, _):
        for k in range(2):
            entry, t = found(2 * j + k, NX)
            part = adj[t]
            tiles[0, j, :, k * B : (k + 1) * B] = jnp.where(entry > 0, part, jnp.zeros_like(part))
        return 0

    def quarter(i, dy, lo=0, n=PAIRS):
        return tiles.at[i, pl.ds(lo, n), q_rows(dy), :]

    hops_x = (1, -1, 2)
    for i, dx in enumerate(hops_x):
        lax.fori_loop(0, PAIRS, functools.partial(pack, i, dx), 0)
        go(remote(send.at[i], quarter(-dx % NX, 0), xs.at[i], xr.at[i], me.at(dx=dx)))

    half = (PAIRS + 1) // 2
    cut = ((0, half), (half, PAIRS - half))

    def tiles_from_x(i):
        dx = hops_x[i]
        spot = quarter(-dx % NX, 0)
        remote(spot, spot, xs.at[i], xr.at[i], me.at(dx=-dx)).wait_recv()
        for way, d in WAYS:
            go(remote(spot, spot, ys.at[i * 4 + way], yr.at[i * 4 + way], me.at(dy=d)))

    def tiles_from_y(i):
        for way, d in WAYS:
            spot = quarter(-hops_x[i] % NX, -d)
            sem = i * 4 + way
            remote(spot, spot, ys.at[sem], yr.at[sem], me.at(dy=-d)).wait_recv()
            part = quarter(-hops_x[i] % NX, -d, *cut[way])
            go(remote(part, part, ys.at[sem + 2], yr.at[sem + 2], me.at(dy=d)))

    def tiles_last(i):
        for way, d in WAYS:
            spot = quarter(-hops_x[i] % NX, 2, *cut[way])
            sem = i * 4 + way + 2
            remote(spot, spot, ys.at[sem], yr.at[sem], me.at(dy=-d)).wait_recv()

    def place_of(hops, side):
        z = lax.rem(me.z + (NZ - hops), NZ)
        return z * NC + (1 - me.c if side else me.c)

    def spread(i, rd, pair):
        rows = []
        for k in range(2):
            entry = jnp.maximum(tab[2 * pair + k, rd] - 1, 0)
            tile = tiles[rd, pair, :, k * B : (k + 1) * B]
            at = pl.ds((2 * i + k) * B, B)
            r = lax.shift_right_logical(entry, 11)
            for row in range(R):
                lhs[row * B : (row + 1) * B, at] = jnp.where(r == row, tile, jnp.zeros_like(tile))
            rows.append((jnp.bitwise_and(entry, 127), at))
        return rows

    def product(layer, step, rd):
        held = blocks[layer]
        for i, (hops, side) in enumerate(STEPS[step]):
            for entry, at in spread(i, rd, place_of(hops, side)):
                rhs[at, :] = held[hops][side][jnp.bitwise_and(entry, 7)]
        n = len(STEPS[step])
        if step == 4:
            for entry, at in spread(n, rd, PAIRS - 1):
                b, q = jnp.bitwise_and(entry, 7), lax.shift_right_logical(entry, 3)
                got = held[0][0][b]
                for hops in range(NZ):
                    for side in range(2):
                        if hops or side:
                            got = jnp.where(q == place_of(hops, side), held[hops][side][b], got)
                rhs[at, :] = got
            n += 1
        width = n * 2 * B
        total = jnp.dot(lhs[:, :width], rhs[:width, :], preferred_element_type=F32)
        acc[rd] = total if step == 0 else acc[rd] + total

    def layer_end(layer, weight, put):
        part, relay_in, relay_out, sums_in, agg, xs, xr, ys, yr = ends[layer]
        halves = lambda k: (pl.ds(k * RC, HC), pl.ds(k * RC + HC, HC))

        def x_far(k):
            rows = pl.ds(k * RC, RC)
            part[2, rows, :] = acc[2, rows, :].astype(BF)
            for way, d in WAYS:
                i = (way * NP + k) * 3
                go(remote(part.at[2, halves(k)[way]], relay_in.at[way, k], xs.at[i], xr.at[i], me.at(dx=d)))

        def x_near(k):
            for way, d in WAYS:
                i = (way * NP + k) * 3 + 1
                rows = halves(k)[1 - way]
                part[d % NX, rows, :] = acc[d % NX, rows, :].astype(BF)
                go(remote(part.at[d % NX, rows], sums_in.at[way, rows], xs.at[i], xr.at[i], me.at(dx=d)))

        def x_relay(k):
            for way, d in WAYS:
                i = (way * NP + k) * 3
                spot = relay_in.at[way, k]
                remote(spot, spot, xs.at[i], xr.at[i], me.at(dx=-d)).wait_recv()
                rows = halves(k)[way]
                relay_out[way, k] = (acc[d % NX, rows, :] + relay_in[way, k].astype(F32)).astype(BF)
                go(remote(relay_out.at[way, k], sums_in.at[way, rows], xs.at[i + 2], xr.at[i + 2], me.at(dx=d)))

        def x_sum(k):
            for way, d in WAYS:
                for j, rows in ((1, halves(k)[1 - way]), (2, halves(k)[way])):
                    i = (way * NP + k) * 3 + j
                    spot = sums_in.at[way, rows]
                    remote(spot, spot, xs.at[i], xr.at[i], me.at(dx=-d)).wait_recv()
            rows = pl.ds(k * RC, RC)
            total = acc[0, rows, :] + sums_in[0, rows, :].astype(F32) + sums_in[1, rows, :].astype(F32)
            agg[me.y, rows, :] = total.astype(BF)
            for way, d in WAYS:
                i = (way * NP + k) * 2
                spot = agg.at[me.y, rows]
                go(remote(spot, spot, ys.at[i], yr.at[i], me.at(dy=d)))

        def y_pass(k):
            for way, d in WAYS:
                i = (way * NP + k) * 2
                spot = agg.at[me.y_of(-d), pl.ds(k * RC, RC)]
                remote(spot, spot, ys.at[i], yr.at[i], me.at(dy=-d)).wait_recv()
                spot = agg.at[me.y_of(-d), halves(k)[way]]
                go(remote(spot, spot, ys.at[i + 1], yr.at[i + 1], me.at(dy=d)))

        def transform(k):
            for way, d in WAYS:
                i = (way * NP + k) * 2 + 1
                spot = agg.at[me.y_of(2), halves(k)[way]]
                remote(spot, spot, ys.at[i], yr.at[i], me.at(dy=-d)).wait_recv()
            total = jnp.zeros((RC, COLS), F32)
            for y in range(NY):
                total += jnp.dot(
                    agg[y, pl.ds(k * RC, RC), :], weight[pl.ds(y * COLS, COLS), :], preferred_element_type=F32
                )
            put(k, total)

        x_far(0)
        for turn in range(NP + 3):
            if turn + 1 < NP:
                x_far(turn + 1)
            if turn < NP:
                x_near(turn)
                x_relay(turn)
            if 0 <= turn - 1 < NP:
                x_sum(turn - 1)
            if 0 <= turn - 2 < NP:
                y_pass(turn - 2)
            if 0 <= turn - 3 < NP:
                transform(turn - 3)

    first = rings[0]
    both = lambda s, k: [first.arrive(way, s, k, s < 2 or (s == 2 and (k < NP // 2) == (way == 0))) for way in range(2)]
    lax.fori_loop(0, PAIRS, keep, 0)
    both(0, 0)
    both(0, 1)
    tiles_from_x(0)
    tiles_from_x(1)
    both(0, 2)
    both(0, 3)
    tiles_from_x(2)
    both(1, 0)
    both(1, 1)
    tiles_from_y(0)
    both(1, 2)
    both(1, 3)
    tiles_from_y(1)
    both(2, 0)
    both(2, 1)
    tiles_from_y(2)
    both(2, 2)
    both(2, 3)
    loads[1].wait()
    for k in range(NP):
        first.arrive(0 if k < NP // 2 else 1, 3, k, False)
    for i in range(3):
        tiles_last(i)

    def layer_one(rd, _):
        for step in range(4):
            product(0, step, rd)
        return 0

    first.from_sibling(*(h for h in range(NZ) if h != 4))
    lax.fori_loop(0, NX, layer_one, 0)
    first.from_sibling(4)
    lax.fori_loop(0, NX, lambda rd, _: product(0, 4, rd) or 0, 0)
    loads[2].wait()
    loads[3].wait()
    second = rings[1]

    def put_hidden(k, total):
        hidden = jnp.maximum(total, 0.0).astype(BF).reshape(PER, B, COLS)
        blocks[1][0][0][pl.ds(k * PER, PER)] = hidden
        second.send_own(k)

    layer_end(0, w1, put_hidden)

    second.run(lambda step, k: product(1, step, k))

    def layer_two(rd, _):
        product(1, 3, rd)
        product(1, 4, rd)
        return 0

    lax.fori_loop(0, NX, layer_two, 0)

    def put_out(k, total):
        done[pl.ds(k * PER, PER)] = total.astype(BF).reshape(PER, B, COLS)

    layer_end(1, w2, put_out)

    slots = [mig[m, me.dom] for m in range(2)]
    for m in range(2):
        leave[m] = done[slots[m]]
    move = remote(leave, came, ms, mr, me.along(1))
    move.start()
    move.wait()
    done[pl.ds(R, 2)] = came[...]
    for r in range(R):
        at = jnp.where(slots[0] == r, R, jnp.where(slots[1] == r, R + 1, r))
        out[pl.ds(r * B, B), :] = done[at]
    for ring in rings:
        ring.finish()
    for copy in started:
        copy.wait_send()


def run_all(tab, mig_slot, features, adjacency, weight_one, weight_two):
    vmem = pl.BlockSpec(memory_space=pltpu.VMEM)
    smem = pl.BlockSpec(memory_space=pltpu.SMEM)
    hbm = pl.BlockSpec(memory_space=pl.ANY)
    dma = pltpu.SemaphoreType.DMA
    return pl.pallas_call(
        whole_kernel,
        name="two_layers",
        out_shape=jax.ShapeDtypeStruct((ROWS, COLS), BF),
        in_specs=[smem, smem, hbm, hbm, hbm, hbm],
        out_specs=vmem,
        scratch_shapes=[pltpu.VMEM((R, B, COLS), BF)] * (4 * NZ)
        + [
            pltpu.VMEM((TILES, B, B), BF),
            pltpu.VMEM((NX, PAIRS, B, 2 * B), BF),
            pltpu.VMEM((3, PAIRS, QROWS, 2 * B), BF),
            pltpu.VMEM((NY * COLS, COLS), BF),
            pltpu.VMEM((NY * COLS, COLS), BF),
            pltpu.VMEM((NX, ROWS, COLS), F32),
            pltpu.VMEM((ROWS, 8 * B), BF),
            pltpu.VMEM((8 * B, COLS), BF),
            pltpu.VMEM((R + 2, B, COLS), BF),
            pltpu.VMEM((2, B, COLS), BF),
            pltpu.VMEM((2, B, COLS), BF),
            dma((4,)),
            dma((3,)),
            dma((3,)),
            dma((12,)),
            dma((12,)),
            dma,
            dma,
        ]
        + ring_scratch() * 2
        + end_scratch() * 2,
        compiler_params=pltpu.CompilerParams(
            collective_id=0, has_side_effects=True, vmem_limit_bytes=60 * 1024 * 1024
        ),
    )(tab, mig_slot.T, features, adjacency, weight_one, weight_two)


def on_device(features, adjacency, tile_src, mig_slot, weight_one, weight_two):
    dom = lax.axis_index("dom")
    z, c = lax.rem(lax.div(dom, NC), NZ), lax.rem(dom, NC)
    grid = tile_src.reshape(NX, NZ, NC, TILES)
    sources = lax.dynamic_slice(grid, (0, z, c, 0), (NX, 1, 1, TILES)).reshape(NX, TILES)
    tab = tables(sources)
    return run_all(
        tab, mig_slot, features.reshape(R, B, COLS), adjacency.reshape(TILES, B, B), weight_one, weight_two
    )


def solution(mesh):
    in_specs = (P("dom", "feat"), P("dom", None, None, None), P(), P(), P(), P())
    return jax.shard_map(
        on_device, mesh=mesh, in_specs=in_specs, out_specs=P("dom", "feat"), check_vma=False
    )
```

```python
import functools

import jax
import jax.numpy as jnp
from jax import lax
from jax.experimental import pallas as pl
from jax.experimental.pallas import tpu as pltpu
from jax.sharding import PartitionSpec as P

B = 128
R = 8
TPB = 16
NX, NZ, NC, NY = 4, 8, 2, 4
NDOM = NX * NZ * NC
COLS = 256
ROWS = R * B
TILES = R * TPB
PAIRS = NZ * NC + 1
SLOTS = 2 * PAIRS
QROWS = B // NY
NP = 4
PER = R // NP
NE = 4
RC = ROWS // NE
HC = RC // 2
MESH = pl.DeviceIdType.MESH
BF, F32 = jnp.bfloat16, jnp.float32
WAYS = ((0, 1), (1, -1))


class Place:
    def __init__(self):
        d = lax.axis_index("dom")
        self.dom = d
        self.y = lax.axis_index("feat")
        self.x = d // (NZ * NC)
        self.z = lax.rem(d // NC, NZ)
        self.c = lax.rem(d, NC)

    def at(self, dx=0, dz=0, sibling=False, dy=0):
        x = lax.rem(self.x + (dx + NX), NX)
        z = lax.rem(self.z + (dz + NZ), NZ)
        c = 1 - self.c if sibling else self.c
        y = lax.rem(self.y + (dy + NY), NY)
        return ((x * NZ + z) * NC + c, y)

    def along(self, by):
        return (lax.rem(self.dom + (by + NDOM), NDOM), self.y)

    def y_of(self, dy):
        return lax.rem(self.y + (dy + NY), NY)


def remote(src, dst, send, recv, device):
    return pltpu.make_async_remote_copy(
        src_ref=src, dst_ref=dst, send_sem=send, recv_sem=recv, device_id=device, device_id_type=MESH
    )


def table_kernel(src_ref, tab_ref):
    x = lax.axis_index("dom") // (NZ * NC)
    t_row = lax.broadcasted_iota(jnp.int32, (1, TILES), 1)
    earlier = lax.broadcasted_iota(jnp.int32, (TILES, TILES), 0) < lax.broadcasted_iota(jnp.int32, (TILES, TILES), 1)
    lane = lax.broadcasted_iota(jnp.int32, (40, 128), 1)
    slot = lax.broadcasted_iota(jnp.int32, (40, TILES), 0)
    total = jnp.zeros((40, 128), F32)

    def ranks(i):
        s = src_ref[pl.ds(lax.rem(x + i, NX), 1), :]
        q = lax.shift_right_logical(s, 3)
        down = jnp.transpose(jnp.broadcast_to(q, (TILES, TILES)))
        same = jnp.where(jnp.logical_and(down == q, earlier), 1.0, 0.0)
        return s, q, jnp.sum(same, axis=0, keepdims=True)

    def column(total, at, s, q, rank, col):
        here = lax.shift_right_logical(q, 4) == col
        regular = jnp.logical_and(here, rank < 1.5)
        more = jnp.logical_and(here, rank > 1.5)
        first = jnp.min(jnp.where(more, t_row, TILES), axis=1, keepdims=True)
        place = jnp.where(
            regular,
            2 * jnp.bitwise_and(q, 15) + rank.astype(jnp.int32),
            jnp.where(more, SLOTS - 2 + jnp.where(t_row > first, 1, 0), -1),
        )
        entry = (1 + t_row * 128 + jnp.bitwise_and(s, 127)).astype(F32)
        found = jnp.sum(jnp.where(slot == place, entry, 0.0), axis=1, keepdims=True)
        return total + jnp.where(lane == at, found, 0.0)

    own = ranks(0)
    for i in range(NX):
        total = column(total, i, *(own if i == 0 else ranks(i)), x)
        total = column(total, NX + i, *own, lax.rem(x + i, NX))
    tab_ref[...] = total.astype(jnp.int32)


def tables(sources):
    vmem = pl.BlockSpec(memory_space=pltpu.VMEM)
    return pl.pallas_call(
        table_kernel,
        name="tile_tables",
        out_shape=jax.ShapeDtypeStruct((40, 128), jnp.int32),
        in_specs=[vmem],
        out_specs=vmem,
    )(sources)


def ring_scratch():
    n = 2 * 4 * NP
    return [pltpu.SemaphoreType.DMA((n,)), pltpu.SemaphoreType.DMA((n,))] + [
        pltpu.SemaphoreType.DMA((NZ + 1,)),
        pltpu.SemaphoreType.DMA((NZ + 1,)),
    ]


def end_scratch():
    return [
        pltpu.VMEM((NX, ROWS, COLS), BF),
        pltpu.VMEM((2, NE, HC, COLS), BF),
        pltpu.VMEM((2, NE, HC, COLS), BF),
        pltpu.VMEM((2, ROWS, COLS), BF),
        pltpu.VMEM((NY, ROWS, COLS), BF),
        pltpu.SemaphoreType.DMA((2 * NE * 3,)),
        pltpu.SemaphoreType.DMA((2 * NE * 3,)),
        pltpu.SemaphoreType.DMA((2 * NE * 2,)),
        pltpu.SemaphoreType.DMA((2 * NE * 2,)),
    ]


class Ring:
    def __init__(self, me, blocks, whole, sems):
        self.me, self.blocks, self.whole = me, blocks, whole
        self.own = lambda k: whole.at[pl.ds(k * PER, PER)]
        self.zs, self.zr, self.ss, self.sr = sems

    def spot(self, hops, side, k):
        return self.blocks[hops % NZ][side].at[pl.ds(k * PER, PER)]

    def source(self, hops, k):
        return self.own(k) if hops % NZ == 0 else self.spot(hops, 0, k)

    def z_copy(self, way, s, k):
        hops = s if way == 0 else -s
        on = s + 1 if way == 0 else -(s + 1)
        i = (way * 4 + s) * NP + k
        up = 1 if way == 0 else -1
        return remote(self.source(hops, k), self.spot(on, 0, k), self.zs.at[i], self.zr.at[i], self.me.at(dz=up))

    def z_arrival(self, way, s, k):
        spot = self.spot(s + 1 if way == 0 else -(s + 1), 0, k)
        i = (way * 4 + s) * NP + k
        return remote(spot, spot, self.zs.at[i], self.zr.at[i], self.me.at(dz=-1 if way == 0 else 1))

    def sib_part(self, part):
        return (4, pl.ds(R // 2 * (part // 8), R // 2)) if part in (4, 8) else (part, pl.ds(0, R))

    def sib_copy(self, part):
        hops, rows = self.sib_part(part)
        src = self.blocks[hops][0].at[rows] if hops else self.whole
        dst = self.blocks[hops][1].at[rows]
        return remote(src, dst, self.ss.at[part], self.sr.at[part], self.me.at(sibling=True))

    def from_sibling(self, *parts):
        for part in parts:
            hops, rows = self.sib_part(part)
            spot = self.blocks[hops][1].at[rows]
            remote(spot, spot, self.ss.at[part], self.sr.at[part], self.me.at(sibling=True)).wait_recv()

    def send_own(self, k):
        for way in range(2):
            self.z_copy(way, 0, k).start()
        if k == NP - 1:
            self.sib_copy(0).start()

    def arrive(self, way, s, k, on):
        self.z_arrival(way, s, k).wait_recv()
        if on:
            self.z_copy(way, s + 1, k).start()

    def share(self, s):
        for part in (s + 1, 7 - s if s < 3 else 8):
            self.sib_copy(part).start()

    def finish(self):
        for way in range(2):
            for s in range(4):
                for k in range(NP):
                    if s < 3 or (k < NP // 2) == (way == 0):
                        self.z_copy(way, s, k).wait_send()
        for part in range(NZ + 1):
            self.sib_copy(part).wait_send()

    def run(self, between):
        each = NX // NP
        for s in range(4):
            if s:
                self.from_sibling(*sorted({s - 1, -(s - 1) % NZ}))

            def turn(k, _, ways, on, s=s):
                for way in ways:
                    self.arrive(way, s, k, on[way])
                if s:
                    for i in range(each):
                        between(s - 1, k * each + i)
                return 0

            halves = ((0, NP // 2), (NP // 2, NP))
            if s < 2:
                lax.fori_loop(0, NP, functools.partial(turn, ways=(0, 1), on=(True, True)), 0)
            else:
                for way, (lo, hi) in enumerate(halves):
                    on = (s == 2 and way == 0, s == 2 and way == 1)
                    ways = (0, 1) if s == 2 else (way,)
                    lax.fori_loop(lo, hi, functools.partial(turn, ways=ways, on=on), 0)
            self.share(s)
        self.from_sibling(3, 5, 4, 8)


STEPS = (
    ((0, 0), (0, 1)),
    ((1, 0), (1, 1), (7, 0), (7, 1)),
    ((2, 0), (2, 1), (6, 0), (6, 1)),
    ((3, 0), (3, 1), (5, 0), (5, 1)),
    ((4, 0), (4, 1)),
)


def whole_kernel(tab, mig, x_ref, adj_ref, w1_ref, w2_ref, out, *refs):
    refs = list(refs)

    def take(n):
        head = refs[:n]
        del refs[:n]
        return head

    flat = [take(2 * NZ) for _ in range(2)]
    blocks = [[f[2 * h : 2 * h + 2] for h in range(NZ)] for f in flat]
    adj, tiles, send, w1, w2, acc, lhs, rhs, done, leave, came = take(11)
    loc, xs, xr, ys, yr, ms, mr = take(7)
    ring_sems = [take(4) for _ in range(2)]
    ends = [take(9) for _ in range(2)]
    me = Place()

    col = pl.ds(pl.multiple_of(me.y * COLS, COLS), COLS)
    loads = [
        pltpu.make_async_copy(adj_ref, adj, loc.at[0]),
        pltpu.make_async_copy(x_ref, blocks[0][0][0], loc.at[1]),
        pltpu.make_async_copy(w1_ref.at[:, col], w1, loc.at[2]),
        pltpu.make_async_copy(w2_ref.at[:, col], w2, loc.at[3]),
    ]
    for load in loads:
        load.start()

    partners = [me.at(dz=1), me.at(dz=-1), me.at(sibling=True), me.at(dy=1), me.at(dy=-1)]
    partners += [me.at(dx=1), me.at(dx=-1), me.at(dx=2), me.along(1), me.along(-1)]
    barrier = pltpu.get_barrier_semaphore()
    for p in partners:
        pl.semaphore_signal(barrier, inc=1, device_id=p, device_id_type=MESH)
    pl.semaphore_wait(barrier, len(partners))

    rings = [
        Ring(me, blocks[0], x_ref, ring_sems[0]),
        Ring(me, blocks[1], blocks[1][0][0], ring_sems[1]),
    ]
    for k in range(NP):
        rings[0].send_own(k)

    started = []

    def go(copy):
        copy.start()
        started.append(copy)

    q_rows = lambda dy: pl.ds(pl.multiple_of(me.y_of(dy) * QROWS, QROWS), QROWS)
    loads[0].wait()

    def found(j, column):
        entry = tab[j, column]
        return entry, jnp.bitwise_and(lax.shift_right_logical(jnp.maximum(entry - 1, 0), 7), TILES - 1)

    def pack(i, dx, j, _):
        for k in range(2):
            entry, t = found(2 * j + k, NX + dx % NX)
            part = adj[t, q_rows(0), :]
            send[i, j, :, k * B : (k + 1) * B] = jnp.where(entry > 0, part, jnp.zeros_like(part))
        return 0

    def keep(j, _):
        for k in range(2):
            entry, t = found(2 * j + k, NX)
            part = adj[t]
            tiles[0, j, :, k * B : (k + 1) * B] = jnp.where(entry > 0, part, jnp.zeros_like(part))
        return 0

    def quarter(i, dy, lo=0, n=PAIRS):
        return tiles.at[i, pl.ds(lo, n), q_rows(dy), :]

    hops_x = (1, -1, 2)
    for i, dx in enumerate(hops_x):
        lax.fori_loop(0, PAIRS, functools.partial(pack, i, dx), 0)
        go(remote(send.at[i], quarter(-dx % NX, 0), xs.at[i], xr.at[i], me.at(dx=dx)))

    half = (PAIRS + 1) // 2
    cut = ((0, half), (half, PAIRS - half))

    def tiles_from_x(i):
        dx = hops_x[i]
        spot = quarter(-dx % NX, 0)
        remote(spot, spot, xs.at[i], xr.at[i], me.at(dx=-dx)).wait_recv()
        for way, d in WAYS:
            go(remote(spot, spot, ys.at[i * 4 + way], yr.at[i * 4 + way], me.at(dy=d)))

    def tiles_from_y(i):
        for way, d in WAYS:
            spot = quarter(-hops_x[i] % NX, -d)
            sem = i * 4 + way
            remote(spot, spot, ys.at[sem], yr.at[sem], me.at(dy=-d)).wait_recv()
            part = quarter(-hops_x[i] % NX, -d, *cut[way])
            go(remote(part, part, ys.at[sem + 2], yr.at[sem + 2], me.at(dy=d)))

    def tiles_last(i):
        for way, d in WAYS:
            spot = quarter(-hops_x[i] % NX, 2, *cut[way])
            sem = i * 4 + way + 2
            remote(spot, spot, ys.at[sem], yr.at[sem], me.at(dy=-d)).wait_recv()

    def place_of(hops, side):
        z = lax.rem(me.z + (NZ - hops), NZ)
        return z * NC + (1 - me.c if side else me.c)

    def spread(i, rd, pair):
        rows = []
        for k in range(2):
            entry = jnp.maximum(tab[2 * pair + k, rd] - 1, 0)
            tile = tiles[rd, pair, :, k * B : (k + 1) * B]
            at = pl.ds((2 * i + k) * B, B)
            r = lax.shift_right_logical(entry, 11)
            for row in range(R):
                lhs[row * B : (row + 1) * B, at] = jnp.where(r == row, tile, jnp.zeros_like(tile))
            rows.append((jnp.bitwise_and(entry, 127), at))
        return rows

    def product(layer, step, rd):
        held = blocks[layer]
        for i, (hops, side) in enumerate(STEPS[step]):
            for entry, at in spread(i, rd, place_of(hops, side)):
                rhs[at, :] = held[hops][side][jnp.bitwise_and(entry, 7)]
        n = len(STEPS[step])
        if step == 4:
            for entry, at in spread(n, rd, PAIRS - 1):
                b, q = jnp.bitwise_and(entry, 7), lax.shift_right_logical(entry, 3)
                got = held[0][0][b]
                for hops in range(NZ):
                    for side in range(2):
                        if hops or side:
                            got = jnp.where(q == place_of(hops, side), held[hops][side][b], got)
                rhs[at, :] = got
            n += 1
        width = n * 2 * B
        total = jnp.dot(lhs[:, :width], rhs[:width, :], preferred_element_type=F32)
        acc[rd] = total if step == 0 else acc[rd] + total

    def layer_end(layer, weight, last, put):
        part, relay_in, relay_out, sums_in, agg, xs, xr, ys, yr = ends[layer]
        halves = lambda k: (pl.ds(k * RC, HC), pl.ds(k * RC + HC, HC))

        def x_far(k):
            rows = pl.ds(k * RC, RC)
            part[2, rows, :] = acc[2, rows, :].astype(BF)
            for way, d in WAYS:
                i = (way * NE + k) * 3
                go(remote(part.at[2, halves(k)[way]], relay_in.at[way, k], xs.at[i], xr.at[i], me.at(dx=d)))

        def x_near(k):
            for way, d in WAYS:
                i = (way * NE + k) * 3 + 1
                rows = halves(k)[1 - way]
                part[d % NX, rows, :] = acc[d % NX, rows, :].astype(BF)
                go(remote(part.at[d % NX, rows], sums_in.at[way, rows], xs.at[i], xr.at[i], me.at(dx=d)))

        def x_relay(k):
            for way, d in WAYS:
                i = (way * NE + k) * 3
                spot = relay_in.at[way, k]
                remote(spot, spot, xs.at[i], xr.at[i], me.at(dx=-d)).wait_recv()
                rows = halves(k)[way]
                relay_out[way, k] = (acc[d % NX, rows, :] + relay_in[way, k].astype(F32)).astype(BF)
                go(remote(relay_out.at[way, k], sums_in.at[way, rows], xs.at[i + 2], xr.at[i + 2], me.at(dx=d)))

        def x_sum(k):
            for way, d in WAYS:
                for j, rows in ((1, halves(k)[1 - way]), (2, halves(k)[way])):
                    i = (way * NE + k) * 3 + j
                    spot = sums_in.at[way, rows]
                    remote(spot, spot, xs.at[i], xr.at[i], me.at(dx=-d)).wait_recv()
            rows = pl.ds(k * RC, RC)
            total = acc[0, rows, :] + sums_in[0, rows, :].astype(F32) + sums_in[1, rows, :].astype(F32)
            agg[me.y, rows, :] = total.astype(BF)
            for way, d in WAYS:
                i = (way * NE + k) * 2
                spot = agg.at[me.y, rows]
                go(remote(spot, spot, ys.at[i], yr.at[i], me.at(dy=d)))

        def y_pass(k):
            for way, d in WAYS:
                i = (way * NE + k) * 2
                spot = agg.at[me.y_of(-d), pl.ds(k * RC, RC)]
                remote(spot, spot, ys.at[i], yr.at[i], me.at(dy=-d)).wait_recv()
                spot = agg.at[me.y_of(-d), halves(k)[way]]
                go(remote(spot, spot, ys.at[i + 1], yr.at[i + 1], me.at(dy=d)))

        def transform(k):
            for way, d in WAYS:
                i = (way * NE + k) * 2 + 1
                spot = agg.at[me.y_of(2), halves(k)[way]]
                remote(spot, spot, ys.at[i], yr.at[i], me.at(dy=-d)).wait_recv()
            total = jnp.zeros((RC, COLS), F32)
            for y in range(NY):
                total += jnp.dot(
                    agg[y, pl.ds(k * RC, RC), :], weight[pl.ds(y * COLS, COLS), :], preferred_element_type=F32
                )
            put(k, total)

        def finish():
            for turn in range(NE + 3):
                if turn < NE:
                    x_relay(turn)
                if turn + 1 < NE:
                    x_near(turn + 1)
                rest(turn)

        def rest(turn):
            if 0 <= turn - 1 < NE:
                x_sum(turn - 1)
            if 0 <= turn - 2 < NE:
                y_pass(turn - 2)
            if 0 <= turn - 3 < NE:
                transform(turn - 3)

        last(2)
        for k in range(NE):
            x_far(k)
        lax.fori_loop(0, 2, lambda i, _: last(2 * i + 1) or 0, 0)
        x_near(0)
        last(0)
        finish()

    first = rings[0]
    both = lambda s, k: [first.arrive(way, s, k, s < 2 or (s == 2 and (k < NP // 2) == (way == 0))) for way in range(2)]
    lax.fori_loop(0, PAIRS, keep, 0)
    tile_turns = [
        lambda: (tiles_from_x(0), tiles_from_x(1)),
        lambda: tiles_from_x(2),
        lambda: tiles_from_y(0),
        lambda: tiles_from_y(1),
        lambda: tiles_from_y(2),
    ]
    for i in range(6):
        for k in range(NP // 2):
            both(i // 2, i % 2 * (NP // 2) + k)
        if i % 2:
            first.share(i // 2)
        if i < len(tile_turns):
            tile_turns[i]()
    for i in range(3):
        tiles_last(i)
    loads[1].wait()

    def products(*steps):
        def one(rd, _):
            for step in steps:
                product(0, step, rd)
            return 0

        lax.fori_loop(0, NX, one, 0)

    first.from_sibling(0, 1, 7)
    products(0, 1)
    first.from_sibling(2, 6)
    products(2)
    for k in range(NP):
        first.arrive(0 if k < NP // 2 else 1, 3, k, False)
    first.share(3)
    first.from_sibling(3, 5, 4, 8)
    loads[2].wait()
    loads[3].wait()
    second = rings[1]

    per = R // NE

    def put_hidden(k, total):
        hidden = jnp.maximum(total, 0.0).astype(BF).reshape(per, B, COLS)
        blocks[1][0][0][pl.ds(k * per, per)] = hidden
        if (k + 1) * per % PER == 0:
            second.send_own((k + 1) * per // PER - 1)

    def last_products(layer):
        def last(rd):
            product(layer, 3, rd)
            product(layer, 4, rd)

        return last

    layer_end(0, w1, last_products(0), put_hidden)

    second.run(lambda step, k: product(1, step, k))

    def put_out(k, total):
        done[pl.ds(k * per, per)] = total.astype(BF).reshape(per, B, COLS)

    layer_end(1, w2, last_products(1), put_out)

    slots = [mig[m, me.dom] for m in range(2)]
    for m in range(2):
        leave[m] = done[slots[m]]
    move = remote(leave, came, ms, mr, me.along(1))
    move.start()
    move.wait()
    done[pl.ds(R, 2)] = came[...]
    for r in range(R):
        at = jnp.where(slots[0] == r, R, jnp.where(slots[1] == r, R + 1, r))
        out[pl.ds(r * B, B), :] = done[at]
    for ring in rings:
        ring.finish()
    for copy in started:
        copy.wait_send()


def run_all(tab, mig_slot, features, adjacency, weight_one, weight_two):
    vmem = pl.BlockSpec(memory_space=pltpu.VMEM)
    smem = pl.BlockSpec(memory_space=pltpu.SMEM)
    hbm = pl.BlockSpec(memory_space=pl.ANY)
    dma = pltpu.SemaphoreType.DMA
    return pl.pallas_call(
        whole_kernel,
        name="two_layers",
        out_shape=jax.ShapeDtypeStruct((ROWS, COLS), BF),
        in_specs=[smem, smem, hbm, hbm, hbm, hbm],
        out_specs=vmem,
        scratch_shapes=[pltpu.VMEM((R, B, COLS), BF)] * (4 * NZ)
        + [
            pltpu.VMEM((TILES, B, B), BF),
            pltpu.VMEM((NX, PAIRS, B, 2 * B), BF),
            pltpu.VMEM((3, PAIRS, QROWS, 2 * B), BF),
            pltpu.VMEM((NY * COLS, COLS), BF),
            pltpu.VMEM((NY * COLS, COLS), BF),
            pltpu.VMEM((NX, ROWS, COLS), F32),
            pltpu.VMEM((ROWS, 8 * B), BF),
            pltpu.VMEM((8 * B, COLS), BF),
            pltpu.VMEM((R + 2, B, COLS), BF),
            pltpu.VMEM((2, B, COLS), BF),
            pltpu.VMEM((2, B, COLS), BF),
            dma((4,)),
            dma((3,)),
            dma((3,)),
            dma((12,)),
            dma((12,)),
            dma,
            dma,
        ]
        + ring_scratch() * 2
        + end_scratch() * 2,
        compiler_params=pltpu.CompilerParams(
            collective_id=0, has_side_effects=True, vmem_limit_bytes=60 * 1024 * 1024
        ),
    )(tab, mig_slot.T, features, adjacency, weight_one, weight_two)


def on_device(features, adjacency, tile_src, mig_slot, weight_one, weight_two):
    dom = lax.axis_index("dom")
    z, c = lax.rem(lax.div(dom, NC), NZ), lax.rem(dom, NC)
    grid = tile_src.reshape(NX, NZ, NC, TILES)
    sources = lax.dynamic_slice(grid, (0, z, c, 0), (NX, 1, 1, TILES)).reshape(NX, TILES)
    tab = tables(sources)
    return run_all(
        tab, mig_slot, features.reshape(R, B, COLS), adjacency.reshape(TILES, B, B), weight_one, weight_two
    )


def solution(mesh):
    in_specs = (P("dom", "feat"), P("dom", None, None, None), P(), P(), P(), P())
    return jax.shard_map(
        on_device, mesh=mesh, in_specs=in_specs, out_specs=P("dom", "feat"), check_vma=False
    )
```

```python
import functools

import jax
import jax.numpy as jnp
from jax import lax
from jax.experimental import pallas as pl
from jax.experimental.pallas import tpu as pltpu
from jax.sharding import PartitionSpec as P

B = 128
R = 8
TPB = 16
NX, NZ, NC, NY = 4, 8, 2, 4
NDOM = NX * NZ * NC
COLS = 256
ROWS = R * B
TILES = R * TPB
PAIRS = NZ * NC + 1
SLOTS = 2 * PAIRS
QROWS = B // NY
NP = 4
PER = R // NP
NE = 4
RC = ROWS // NE
HC = RC // 2
MESH = pl.DeviceIdType.MESH
BF, F32 = jnp.bfloat16, jnp.float32
WAYS = ((0, 1), (1, -1))


class Place:
    def __init__(self):
        d = lax.axis_index("dom")
        self.dom = d
        self.y = lax.axis_index("feat")
        self.x = d // (NZ * NC)
        self.z = lax.rem(d // NC, NZ)
        self.c = lax.rem(d, NC)

    def at(self, dx=0, dz=0, sibling=False, dy=0):
        x = lax.rem(self.x + (dx + NX), NX)
        z = lax.rem(self.z + (dz + NZ), NZ)
        c = 1 - self.c if sibling else self.c
        y = lax.rem(self.y + (dy + NY), NY)
        return ((x * NZ + z) * NC + c, y)

    def along(self, by):
        return (lax.rem(self.dom + (by + NDOM), NDOM), self.y)

    def y_of(self, dy):
        return lax.rem(self.y + (dy + NY), NY)


def remote(src, dst, send, recv, device):
    return pltpu.make_async_remote_copy(
        src_ref=src, dst_ref=dst, send_sem=send, recv_sem=recv, device_id=device, device_id_type=MESH
    )


def make_tables(src_ref, tab_ref):
    x = lax.axis_index("dom") // (NZ * NC)
    t_row = lax.broadcasted_iota(jnp.int32, (1, TILES), 1)
    earlier = lax.broadcasted_iota(jnp.int32, (TILES, TILES), 0) < lax.broadcasted_iota(jnp.int32, (TILES, TILES), 1)
    lane = lax.broadcasted_iota(jnp.int32, (40, 128), 1)
    slot = lax.broadcasted_iota(jnp.int32, (40, TILES), 0)
    total = jnp.zeros((40, 128), jnp.int32)

    def ranks(i):
        s = src_ref[pl.ds(lax.rem(x + i, NX), 1), :]
        q = lax.shift_right_logical(s, 3)
        down = jnp.transpose(jnp.broadcast_to(q, (TILES, TILES)))
        same = jnp.where(jnp.logical_and(down == q, earlier), 1, 0)
        return s, q, jnp.sum(same, axis=0, keepdims=True)

    def column(total, at, s, q, rank, col):
        here = lax.shift_right_logical(q, 4) == col
        regular = jnp.logical_and(here, rank < 2)
        more = jnp.logical_and(here, rank > 1)
        first = jnp.min(jnp.where(more, t_row, TILES), axis=1, keepdims=True)
        place = jnp.where(
            regular,
            2 * jnp.bitwise_and(q, 15) + rank,
            jnp.where(more, SLOTS - 2 + jnp.where(t_row > first, 1, 0), -1),
        )
        entry = 1 + t_row * 128 + jnp.bitwise_and(s, 127)
        found = jnp.sum(jnp.where(slot == place, entry, 0), axis=1, keepdims=True)
        return total + jnp.where(lane == at, found, 0)

    own = ranks(0)
    for i in range(NX):
        total = column(total, i, *(own if i == 0 else ranks(i)), x)
        total = column(total, NX + i, *own, lax.rem(x + i, NX))
    tab_ref[...] = total


def ring_scratch():
    n = 2 * 4 * NP
    return [pltpu.SemaphoreType.DMA((n,)), pltpu.SemaphoreType.DMA((n,))] + [
        pltpu.SemaphoreType.DMA((NZ + 1,)),
        pltpu.SemaphoreType.DMA((NZ + 1,)),
    ]


def end_scratch():
    return [
        pltpu.VMEM((NX, ROWS, COLS), BF),
        pltpu.VMEM((2, NE, HC, COLS), BF),
        pltpu.VMEM((2, NE, HC, COLS), BF),
        pltpu.VMEM((2, ROWS, COLS), BF),
        pltpu.VMEM((NY, ROWS, COLS), BF),
        pltpu.SemaphoreType.DMA((2 * NE * 3,)),
        pltpu.SemaphoreType.DMA((2 * NE * 3,)),
        pltpu.SemaphoreType.DMA((2 * NE * 2,)),
        pltpu.SemaphoreType.DMA((2 * NE * 2,)),
    ]


class Ring:
    def __init__(self, me, blocks, whole, sems):
        self.me, self.blocks, self.whole = me, blocks, whole
        self.own = lambda k: whole.at[pl.ds(k * PER, PER)]
        self.zs, self.zr, self.ss, self.sr = sems

    def spot(self, hops, side, k):
        return self.blocks[hops % NZ][side].at[pl.ds(k * PER, PER)]

    def source(self, hops, k):
        return self.own(k) if hops % NZ == 0 else self.spot(hops, 0, k)

    def z_copy(self, way, s, k):
        hops = s if way == 0 else -s
        on = s + 1 if way == 0 else -(s + 1)
        i = (way * 4 + s) * NP + k
        up = 1 if way == 0 else -1
        return remote(self.source(hops, k), self.spot(on, 0, k), self.zs.at[i], self.zr.at[i], self.me.at(dz=up))

    def z_arrival(self, way, s, k):
        spot = self.spot(s + 1 if way == 0 else -(s + 1), 0, k)
        i = (way * 4 + s) * NP + k
        return remote(spot, spot, self.zs.at[i], self.zr.at[i], self.me.at(dz=-1 if way == 0 else 1))

    def sib_part(self, part):
        return (4, pl.ds(R // 2 * (part // 8), R // 2)) if part in (4, 8) else (part, pl.ds(0, R))

    def sib_copy(self, part):
        hops, rows = self.sib_part(part)
        src = self.blocks[hops][0].at[rows] if hops else self.whole
        dst = self.blocks[hops][1].at[rows]
        return remote(src, dst, self.ss.at[part], self.sr.at[part], self.me.at(sibling=True))

    def from_sibling(self, *parts):
        for part in parts:
            hops, rows = self.sib_part(part)
            spot = self.blocks[hops][1].at[rows]
            remote(spot, spot, self.ss.at[part], self.sr.at[part], self.me.at(sibling=True)).wait_recv()

    def send_own(self, k):
        for way in range(2):
            self.z_copy(way, 0, k).start()
        if k == NP - 1:
            self.sib_copy(0).start()

    def arrive(self, way, s, k, on):
        self.z_arrival(way, s, k).wait_recv()
        if on:
            self.z_copy(way, s + 1, k).start()

    def share(self, s):
        for part in (s + 1, 7 - s if s < 3 else 8):
            self.sib_copy(part).start()

    def finish(self):
        for way in range(2):
            for s in range(4):
                for k in range(NP):
                    if s < 3 or (k < NP // 2) == (way == 0):
                        self.z_copy(way, s, k).wait_send()
        for part in range(NZ + 1):
            self.sib_copy(part).wait_send()

    def run(self, between):
        each = NX // NP
        for s in range(4):
            if s:
                self.from_sibling(*sorted({s - 1, -(s - 1) % NZ}))

            def turn(k, _, ways, on, s=s):
                for way in ways:
                    self.arrive(way, s, k, on[way])
                if s:
                    for i in range(each):
                        between(s - 1, k * each + i)
                return 0

            halves = ((0, NP // 2), (NP // 2, NP))
            if s < 2:
                lax.fori_loop(0, NP, functools.partial(turn, ways=(0, 1), on=(True, True)), 0)
            else:
                for way, (lo, hi) in enumerate(halves):
                    on = (s == 2 and way == 0, s == 2 and way == 1)
                    ways = (0, 1) if s == 2 else (way,)
                    lax.fori_loop(lo, hi, functools.partial(turn, ways=ways, on=on), 0)
            self.share(s)
        self.from_sibling(3, 5, 4, 8)


STEPS = (
    ((0, 0), (0, 1)),
    ((1, 0), (1, 1), (7, 0), (7, 1)),
    ((2, 0), (2, 1), (6, 0), (6, 1)),
    ((3, 0), (3, 1), (5, 0), (5, 1)),
    ((4, 0), (4, 1)),
)


def whole_kernel(sources, mig, x_ref, adj_ref, w1_ref, w2_ref, out, *refs):
    refs = list(refs)

    def take(n):
        head = refs[:n]
        del refs[:n]
        return head

    flat = [take(2 * NZ) for _ in range(2)]
    blocks = [[f[2 * h : 2 * h + 2] for h in range(NZ)] for f in flat]
    adj, tiles, send, w1, w2, acc, lhs, rhs, done, leave, came = take(11)
    loc, xs, xr, ys, yr, ms, mr = take(7)
    made, tab = take(2)
    ring_sems = [take(4) for _ in range(2)]
    ends = [take(9) for _ in range(2)]
    me = Place()

    col = pl.ds(pl.multiple_of(me.y * COLS, COLS), COLS)
    loads = [
        pltpu.make_async_copy(adj_ref, adj, loc.at[0]),
        pltpu.make_async_copy(x_ref, blocks[0][0][0], loc.at[1]),
        pltpu.make_async_copy(w1_ref.at[:, col], w1, loc.at[2]),
        pltpu.make_async_copy(w2_ref.at[:, col], w2, loc.at[3]),
    ]
    for load in loads:
        load.start()

    partners = [me.at(dz=1), me.at(dz=-1), me.at(sibling=True), me.at(dy=1), me.at(dy=-1)]
    partners += [me.at(dx=1), me.at(dx=-1), me.at(dx=2), me.along(1), me.along(-1)]
    barrier = pltpu.get_barrier_semaphore()
    for p in partners:
        pl.semaphore_signal(barrier, inc=1, device_id=p, device_id_type=MESH)
    pl.semaphore_wait(barrier, len(partners))

    rings = [
        Ring(me, blocks[0], x_ref, ring_sems[0]),
        Ring(me, blocks[1], blocks[1][0][0], ring_sems[1]),
    ]
    for k in range(NP):
        rings[0].send_own(k)

    started = []

    def go(copy):
        copy.start()
        started.append(copy)

    q_rows = lambda dy: pl.ds(pl.multiple_of(me.y_of(dy) * QROWS, QROWS), QROWS)
    make_tables(sources, made)
    to_scalars = pltpu.make_async_copy(made, tab, loc.at[4])
    to_scalars.start()
    to_scalars.wait()
    loads[0].wait()

    def found(j, column):
        entry = tab[j, column]
        return entry, jnp.bitwise_and(lax.shift_right_logical(jnp.maximum(entry - 1, 0), 7), TILES - 1)

    def pack(i, dx, j, _):
        for k in range(2):
            entry, t = found(2 * j + k, NX + dx % NX)
            part = adj[t, q_rows(0), :]
            send[i, j, :, k * B : (k + 1) * B] = jnp.where(entry > 0, part, jnp.zeros_like(part))
        return 0

    def keep(j, _):
        for k in range(2):
            entry, t = found(2 * j + k, NX)
            part = adj[t]
            tiles[0, j, :, k * B : (k + 1) * B] = jnp.where(entry > 0, part, jnp.zeros_like(part))
        return 0

    def quarter(i, dy, lo=0, n=PAIRS):
        return tiles.at[i, pl.ds(lo, n), q_rows(dy), :]

    hops_x = (1, -1, 2)
    for i, dx in enumerate(hops_x):
        lax.fori_loop(0, PAIRS, functools.partial(pack, i, dx), 0)
        go(remote(send.at[i], quarter(-dx % NX, 0), xs.at[i], xr.at[i], me.at(dx=dx)))

    half = (PAIRS + 1) // 2
    cut = ((0, half), (half, PAIRS - half))

    def tiles_from_x(i):
        dx = hops_x[i]
        spot = quarter(-dx % NX, 0)
        remote(spot, spot, xs.at[i], xr.at[i], me.at(dx=-dx)).wait_recv()
        for way, d in WAYS:
            go(remote(spot, spot, ys.at[i * 4 + way], yr.at[i * 4 + way], me.at(dy=d)))

    def tiles_from_y(i):
        for way, d in WAYS:
            spot = quarter(-hops_x[i] % NX, -d)
            sem = i * 4 + way
            remote(spot, spot, ys.at[sem], yr.at[sem], me.at(dy=-d)).wait_recv()
            part = quarter(-hops_x[i] % NX, -d, *cut[way])
            go(remote(part, part, ys.at[sem + 2], yr.at[sem + 2], me.at(dy=d)))

    def tiles_last(i):
        for way, d in WAYS:
            spot = quarter(-hops_x[i] % NX, 2, *cut[way])
            sem = i * 4 + way + 2
            remote(spot, spot, ys.at[sem], yr.at[sem], me.at(dy=-d)).wait_recv()

    def place_of(hops, side):
        z = lax.rem(me.z + (NZ - hops), NZ)
        return z * NC + (1 - me.c if side else me.c)

    def spread(i, rd, pair):
        rows = []
        for k in range(2):
            entry = jnp.maximum(tab[2 * pair + k, rd] - 1, 0)
            tile = tiles[rd, pair, :, k * B : (k + 1) * B]
            at = pl.ds((2 * i + k) * B, B)
            r = lax.shift_right_logical(entry, 11)
            for row in range(R):
                lhs[row * B : (row + 1) * B, at] = jnp.where(r == row, tile, jnp.zeros_like(tile))
            rows.append((jnp.bitwise_and(entry, 127), at))
        return rows

    def product(layer, step, rd):
        held = blocks[layer]
        for i, (hops, side) in enumerate(STEPS[step]):
            for entry, at in spread(i, rd, place_of(hops, side)):
                rhs[at, :] = held[hops][side][jnp.bitwise_and(entry, 7)]
        n = len(STEPS[step])
        if step == 4:
            for entry, at in spread(n, rd, PAIRS - 1):
                b, q = jnp.bitwise_and(entry, 7), lax.shift_right_logical(entry, 3)
                got = held[0][0][b]
                for hops in range(NZ):
                    for side in range(2):
                        if hops or side:
                            got = jnp.where(q == place_of(hops, side), held[hops][side][b], got)
                rhs[at, :] = got
            n += 1
        width = n * 2 * B
        total = jnp.dot(lhs[:, :width], rhs[:width, :], preferred_element_type=F32)
        acc[rd] = total if step == 0 else acc[rd] + total

    def layer_end(layer, weight, last, put):
        part, relay_in, relay_out, sums_in, agg, xs, xr, ys, yr = ends[layer]
        halves = lambda k: (pl.ds(k * RC, HC), pl.ds(k * RC + HC, HC))

        def x_far(k):
            rows = pl.ds(k * RC, RC)
            part[2, rows, :] = acc[2, rows, :].astype(BF)
            for way, d in WAYS:
                i = (way * NE + k) * 3
                go(remote(part.at[2, halves(k)[way]], relay_in.at[way, k], xs.at[i], xr.at[i], me.at(dx=d)))

        def x_near(k):
            for way, d in WAYS:
                i = (way * NE + k) * 3 + 1
                rows = halves(k)[1 - way]
                part[d % NX, rows, :] = acc[d % NX, rows, :].astype(BF)
                go(remote(part.at[d % NX, rows], sums_in.at[way, rows], xs.at[i], xr.at[i], me.at(dx=d)))

        def x_relay(k):
            for way, d in WAYS:
                i = (way * NE + k) * 3
                spot = relay_in.at[way, k]
                remote(spot, spot, xs.at[i], xr.at[i], me.at(dx=-d)).wait_recv()
                rows = halves(k)[way]
                relay_out[way, k] = (acc[d % NX, rows, :] + relay_in[way, k].astype(F32)).astype(BF)
                go(remote(relay_out.at[way, k], sums_in.at[way, rows], xs.at[i + 2], xr.at[i + 2], me.at(dx=d)))

        def x_sum(k):
            for way, d in WAYS:
                for j, rows in ((1, halves(k)[1 - way]), (2, halves(k)[way])):
                    i = (way * NE + k) * 3 + j
                    spot = sums_in.at[way, rows]
                    remote(spot, spot, xs.at[i], xr.at[i], me.at(dx=-d)).wait_recv()
            rows = pl.ds(k * RC, RC)
            total = acc[0, rows, :] + sums_in[0, rows, :].astype(F32) + sums_in[1, rows, :].astype(F32)
            agg[me.y, rows, :] = total.astype(BF)
            for way, d in WAYS:
                i = (way * NE + k) * 2
                spot = agg.at[me.y, rows]
                go(remote(spot, spot, ys.at[i], yr.at[i], me.at(dy=d)))

        def y_pass(k):
            for way, d in WAYS:
                i = (way * NE + k) * 2
                spot = agg.at[me.y_of(-d), pl.ds(k * RC, RC)]
                remote(spot, spot, ys.at[i], yr.at[i], me.at(dy=-d)).wait_recv()
                spot = agg.at[me.y_of(-d), halves(k)[way]]
                go(remote(spot, spot, ys.at[i + 1], yr.at[i + 1], me.at(dy=d)))

        def transform(k):
            for way, d in WAYS:
                i = (way * NE + k) * 2 + 1
                spot = agg.at[me.y_of(2), halves(k)[way]]
                remote(spot, spot, ys.at[i], yr.at[i], me.at(dy=-d)).wait_recv()
            total = jnp.zeros((RC, COLS), F32)
            for y in range(NY):
                total += jnp.dot(
                    agg[y, pl.ds(k * RC, RC), :], weight[pl.ds(y * COLS, COLS), :], preferred_element_type=F32
                )
            put(k, total)

        def finish():
            for turn in range(NE + 3):
                if turn < NE:
                    x_relay(turn)
                if turn + 1 < NE:
                    x_near(turn + 1)
                rest(turn)

        def rest(turn):
            if 0 <= turn - 1 < NE:
                x_sum(turn - 1)
            if 0 <= turn - 2 < NE:
                y_pass(turn - 2)
            if 0 <= turn - 3 < NE:
                transform(turn - 3)

        last(2)
        for k in range(NE):
            x_far(k)
        lax.fori_loop(0, 2, lambda i, _: last(2 * i + 1) or 0, 0)
        x_near(0)
        last(0)
        finish()

    first = rings[0]
    both = lambda s, k: [first.arrive(way, s, k, s < 2 or (s == 2 and (k < NP // 2) == (way == 0))) for way in range(2)]
    lax.fori_loop(0, PAIRS, keep, 0)
    tile_turns = [
        lambda: (tiles_from_x(0), tiles_from_x(1)),
        lambda: tiles_from_x(2),
        lambda: tiles_from_y(0),
        lambda: tiles_from_y(1),
        lambda: tiles_from_y(2),
    ]
    for i in range(6):
        for k in range(NP // 2):
            both(i // 2, i % 2 * (NP // 2) + k)
        if i % 2:
            first.share(i // 2)
        if i < len(tile_turns):
            tile_turns[i]()
    for i in range(3):
        tiles_last(i)
    loads[1].wait()

    def products(*steps):
        def one(rd, _):
            for step in steps:
                product(0, step, rd)
            return 0

        lax.fori_loop(0, NX, one, 0)

    first.from_sibling(0, 1, 7)
    products(0, 1)
    first.from_sibling(2, 6)
    products(2)
    for k in range(NP):
        first.arrive(0 if k < NP // 2 else 1, 3, k, False)
    first.share(3)
    first.from_sibling(3, 5, 4, 8)
    loads[2].wait()
    loads[3].wait()
    second = rings[1]

    per = R // NE

    def put_hidden(k, total):
        hidden = jnp.maximum(total, 0.0).astype(BF).reshape(per, B, COLS)
        blocks[1][0][0][pl.ds(k * per, per)] = hidden
        if (k + 1) * per % PER == 0:
            second.send_own((k + 1) * per // PER - 1)

    def last_products(layer):
        def last(rd):
            product(layer, 3, rd)
            product(layer, 4, rd)

        return last

    layer_end(0, w1, last_products(0), put_hidden)

    second.run(lambda step, k: product(1, step, k))

    def put_out(k, total):
        done[pl.ds(k * per, per)] = total.astype(BF).reshape(per, B, COLS)

    layer_end(1, w2, last_products(1), put_out)

    slots = [mig[m, me.dom] for m in range(2)]
    for m in range(2):
        leave[m] = done[slots[m]]
    move = remote(leave, came, ms, mr, me.along(1))
    move.start()
    move.wait()
    done[pl.ds(R, 2)] = came[...]
    for r in range(R):
        at = jnp.where(slots[0] == r, R, jnp.where(slots[1] == r, R + 1, r))
        out[pl.ds(r * B, B), :] = done[at]
    for ring in rings:
        ring.finish()
    for copy in started:
        copy.wait_send()


def run_all(sources, mig_slot, features, adjacency, weight_one, weight_two):
    vmem = pl.BlockSpec(memory_space=pltpu.VMEM)
    smem = pl.BlockSpec(memory_space=pltpu.SMEM)
    hbm = pl.BlockSpec(memory_space=pl.ANY)
    dma = pltpu.SemaphoreType.DMA
    return pl.pallas_call(
        whole_kernel,
        name="two_layers",
        out_shape=jax.ShapeDtypeStruct((ROWS, COLS), BF),
        in_specs=[vmem, smem, hbm, hbm, hbm, hbm],
        out_specs=vmem,
        scratch_shapes=[pltpu.VMEM((R, B, COLS), BF)] * (4 * NZ)
        + [
            pltpu.VMEM((TILES, B, B), BF),
            pltpu.VMEM((NX, PAIRS, B, 2 * B), BF),
            pltpu.VMEM((3, PAIRS, QROWS, 2 * B), BF),
            pltpu.VMEM((NY * COLS, COLS), BF),
            pltpu.VMEM((NY * COLS, COLS), BF),
            pltpu.VMEM((NX, ROWS, COLS), F32),
            pltpu.VMEM((ROWS, 8 * B), BF),
            pltpu.VMEM((8 * B, COLS), BF),
            pltpu.VMEM((R + 2, B, COLS), BF),
            pltpu.VMEM((2, B, COLS), BF),
            pltpu.VMEM((2, B, COLS), BF),
            dma((5,)),
            dma((3,)),
            dma((3,)),
            dma((12,)),
            dma((12,)),
            dma,
            dma,
            pltpu.VMEM((40, 128), jnp.int32),
            pltpu.SMEM((40, 128), jnp.int32),
        ]
        + ring_scratch() * 2
        + end_scratch() * 2,
        compiler_params=pltpu.CompilerParams(
            collective_id=0, has_side_effects=True, vmem_limit_bytes=60 * 1024 * 1024
        ),
    )(sources, mig_slot.T, features, adjacency, weight_one, weight_two)


def on_device(features, adjacency, tile_src, mig_slot, weight_one, weight_two):
    dom = lax.axis_index("dom")
    z, c = lax.rem(lax.div(dom, NC), NZ), lax.rem(dom, NC)
    grid = tile_src.reshape(NX, NZ, NC, TILES)
    sources = lax.dynamic_slice(grid, (0, z, c, 0), (NX, 1, 1, TILES)).reshape(NX, TILES)
    return run_all(
        sources, mig_slot, features.reshape(R, B, COLS), adjacency.reshape(TILES, B, B), weight_one, weight_two
    )


def solution(mesh):
    in_specs = (P("dom", "feat"), P("dom", None, None, None), P(), P(), P(), P())
    return jax.shard_map(
        on_device, mesh=mesh, in_specs=in_specs, out_specs=P("dom", "feat"), check_vma=False
    )
```

```python
import functools

import jax
import jax.numpy as jnp
from jax import lax
from jax.experimental import pallas as pl
from jax.experimental.pallas import tpu as pltpu
from jax.sharding import PartitionSpec as P

B = 128
R = 8
TPB = 16
NX, NZ, NC, NY = 4, 8, 2, 4
NDOM = NX * NZ * NC
COLS = 256
ROWS = R * B
TILES = R * TPB
PAIRS = NZ * NC + 1
SLOTS = 2 * PAIRS
QROWS = B // NY
NP = 4
PER = R // NP
NE = 4
RC = ROWS // NE
HC = RC // 2
MESH = pl.DeviceIdType.MESH
BF, F32 = jnp.bfloat16, jnp.float32
WAYS = ((0, 1), (1, -1))


class Place:
    def __init__(self):
        d = lax.axis_index("dom")
        self.dom = d
        self.y = lax.axis_index("feat")
        self.x = d // (NZ * NC)
        self.z = lax.rem(d // NC, NZ)
        self.c = lax.rem(d, NC)

    def at(self, dx=0, dz=0, sibling=False, dy=0):
        x = lax.rem(self.x + (dx + NX), NX)
        z = lax.rem(self.z + (dz + NZ), NZ)
        c = 1 - self.c if sibling else self.c
        y = lax.rem(self.y + (dy + NY), NY)
        return ((x * NZ + z) * NC + c, y)

    def along(self, by):
        return (lax.rem(self.dom + (by + NDOM), NDOM), self.y)

    def y_of(self, dy):
        return lax.rem(self.y + (dy + NY), NY)


def remote(src, dst, send, recv, device):
    return pltpu.make_async_remote_copy(
        src_ref=src, dst_ref=dst, send_sem=send, recv_sem=recv, device_id=device, device_id_type=MESH
    )


def make_tables(src_ref, tab_ref):
    x = lax.axis_index("dom") // (NZ * NC)
    t_row = lax.broadcasted_iota(jnp.int32, (1, TILES), 1)
    earlier = lax.broadcasted_iota(jnp.int32, (TILES, TILES), 0) < lax.broadcasted_iota(jnp.int32, (TILES, TILES), 1)
    lane = lax.broadcasted_iota(jnp.int32, (40, 128), 1)
    slot = lax.broadcasted_iota(jnp.int32, (40, TILES), 0)
    total = jnp.zeros((40, 128), jnp.int32)

    def ranks(i):
        s = src_ref[pl.ds(lax.rem(x + i, NX), 1), :]
        q = lax.shift_right_logical(s, 3)
        down = jnp.transpose(jnp.broadcast_to(q, (TILES, TILES)))
        same = jnp.where(jnp.logical_and(down == q, earlier), 1, 0)
        return s, q, jnp.sum(same, axis=0, keepdims=True)

    def column(total, at, s, q, rank, col):
        here = lax.shift_right_logical(q, 4) == col
        regular = jnp.logical_and(here, rank < 2)
        more = jnp.logical_and(here, rank > 1)
        first = jnp.min(jnp.where(more, t_row, TILES), axis=1, keepdims=True)
        place = jnp.where(
            regular,
            2 * jnp.bitwise_and(q, 15) + rank,
            jnp.where(more, SLOTS - 2 + jnp.where(t_row > first, 1, 0), -1),
        )
        entry = 1 + t_row * 128 + jnp.bitwise_and(s, 127)
        found = jnp.sum(jnp.where(slot == place, entry, 0), axis=1, keepdims=True)
        return total + jnp.where(lane == at, found, 0)

    own = ranks(0)
    for i in range(NX):
        total = column(total, i, *(own if i == 0 else ranks(i)), x)
        total = column(total, NX + i, *own, lax.rem(x + i, NX))
    tab_ref[...] = total


def ring_scratch():
    n = 2 * 4 * NP
    return [pltpu.SemaphoreType.DMA((n,)), pltpu.SemaphoreType.DMA((n,))] + [
        pltpu.SemaphoreType.DMA((NZ + 1,)),
        pltpu.SemaphoreType.DMA((NZ + 1,)),
    ]


def end_scratch():
    return [
        pltpu.VMEM((NX, ROWS, COLS), BF),
        pltpu.VMEM((2, NE, HC, COLS), BF),
        pltpu.VMEM((2, NE, HC, COLS), BF),
        pltpu.VMEM((2, ROWS, COLS), BF),
        pltpu.VMEM((NY, ROWS, COLS), BF),
        pltpu.SemaphoreType.DMA((2 * NE * 3,)),
        pltpu.SemaphoreType.DMA((2 * NE * 3,)),
        pltpu.SemaphoreType.DMA((2 * NE * 2,)),
        pltpu.SemaphoreType.DMA((2 * NE * 2,)),
    ]


class Ring:
    def __init__(self, me, blocks, whole, sems):
        self.me, self.blocks, self.whole = me, blocks, whole
        self.own = lambda k: whole.at[pl.ds(k * PER, PER)]
        self.zs, self.zr, self.ss, self.sr = sems

    def spot(self, hops, side, k):
        return self.blocks[hops % NZ][side].at[pl.ds(k * PER, PER)]

    def source(self, hops, k):
        return self.own(k) if hops % NZ == 0 else self.spot(hops, 0, k)

    def z_copy(self, way, s, k):
        hops = s if way == 0 else -s
        on = s + 1 if way == 0 else -(s + 1)
        i = (way * 4 + s) * NP + k
        up = 1 if way == 0 else -1
        return remote(self.source(hops, k), self.spot(on, 0, k), self.zs.at[i], self.zr.at[i], self.me.at(dz=up))

    def z_arrival(self, way, s, k):
        spot = self.spot(s + 1 if way == 0 else -(s + 1), 0, k)
        i = (way * 4 + s) * NP + k
        return remote(spot, spot, self.zs.at[i], self.zr.at[i], self.me.at(dz=-1 if way == 0 else 1))

    def sib_part(self, part):
        return (4, pl.ds(R // 2 * (part // 8), R // 2)) if part in (4, 8) else (part, pl.ds(0, R))

    def sib_copy(self, part):
        hops, rows = self.sib_part(part)
        src = self.blocks[hops][0].at[rows] if hops else self.whole
        dst = self.blocks[hops][1].at[rows]
        return remote(src, dst, self.ss.at[part], self.sr.at[part], self.me.at(sibling=True))

    def from_sibling(self, *parts):
        for part in parts:
            hops, rows = self.sib_part(part)
            spot = self.blocks[hops][1].at[rows]
            remote(spot, spot, self.ss.at[part], self.sr.at[part], self.me.at(sibling=True)).wait_recv()

    def send_own(self, k):
        for way in range(2):
            self.z_copy(way, 0, k).start()
        if k == NP - 1:
            self.sib_copy(0).start()

    def arrive(self, way, s, k, on):
        self.z_arrival(way, s, k).wait_recv()
        if on:
            self.z_copy(way, s + 1, k).start()

    def share(self, s):
        for part in (s + 1, 7 - s if s < 3 else 8):
            self.sib_copy(part).start()

    def finish(self):
        for way in range(2):
            for s in range(4):
                for k in range(NP):
                    if s < 3 or (k < NP // 2) == (way == 0):
                        self.z_copy(way, s, k).wait_send()
        for part in range(NZ + 1):
            self.sib_copy(part).wait_send()

    def run(self, between):
        each = NX // NP
        for s in range(4):
            if s:
                self.from_sibling(*sorted({s - 1, -(s - 1) % NZ}))

            def turn(k, _, ways, on, s=s):
                for way in ways:
                    self.arrive(way, s, k, on[way])
                if s:
                    for i in range(each):
                        between(s - 1, k * each + i)
                return 0

            halves = ((0, NP // 2), (NP // 2, NP))
            if s < 2:
                lax.fori_loop(0, NP, functools.partial(turn, ways=(0, 1), on=(True, True)), 0)
            else:
                for way, (lo, hi) in enumerate(halves):
                    on = (s == 2 and way == 0, s == 2 and way == 1)
                    ways = (0, 1) if s == 2 else (way,)
                    lax.fori_loop(lo, hi, functools.partial(turn, ways=ways, on=on), 0)
            self.share(s)
        self.from_sibling(3, 5)


STEPS = (
    ((0, 0), (0, 1)),
    ((1, 0), (1, 1), (7, 0), (7, 1)),
    ((2, 0), (2, 1), (6, 0), (6, 1)),
    ((3, 0), (3, 1), (5, 0), (5, 1)),
    ((4, 0), (4, 1)),
)


def whole_kernel(sources, mig, x_ref, adj_ref, w1_ref, w2_ref, out, *refs):
    refs = list(refs)

    def take(n):
        head = refs[:n]
        del refs[:n]
        return head

    flat = [take(2 * NZ) for _ in range(2)]
    blocks = [[f[2 * h : 2 * h + 2] for h in range(NZ)] for f in flat]
    adj, tiles, send, w1, w2, acc, lhs, rhs, done, leave, came = take(11)
    loc, xs, xr, ys, yr, ms, mr = take(7)
    made, tab = take(2)
    ring_sems = [take(4) for _ in range(2)]
    ends = [take(9) for _ in range(2)]
    me = Place()

    col = pl.ds(pl.multiple_of(me.y * COLS, COLS), COLS)
    loads = [
        pltpu.make_async_copy(adj_ref, adj, loc.at[0]),
        pltpu.make_async_copy(x_ref, blocks[0][0][0], loc.at[1]),
        pltpu.make_async_copy(w1_ref.at[:, col], w1, loc.at[2]),
        pltpu.make_async_copy(w2_ref.at[:, col], w2, loc.at[3]),
    ]
    for load in loads:
        load.start()

    partners = [me.at(dz=1), me.at(dz=-1), me.at(sibling=True), me.at(dy=1), me.at(dy=-1)]
    partners += [me.at(dx=1), me.at(dx=-1), me.at(dx=2), me.along(1), me.along(-1)]
    barrier = pltpu.get_barrier_semaphore()
    for p in partners:
        pl.semaphore_signal(barrier, inc=1, device_id=p, device_id_type=MESH)
    pl.semaphore_wait(barrier, len(partners))

    rings = [
        Ring(me, blocks[0], x_ref, ring_sems[0]),
        Ring(me, blocks[1], blocks[1][0][0], ring_sems[1]),
    ]
    for k in range(NP):
        rings[0].send_own(k)

    started = []

    def go(copy):
        copy.start()
        started.append(copy)

    q_rows = lambda dy: pl.ds(pl.multiple_of(me.y_of(dy) * QROWS, QROWS), QROWS)
    make_tables(sources, made)
    to_scalars = pltpu.make_async_copy(made, tab, loc.at[4])
    to_scalars.start()
    to_scalars.wait()
    loads[0].wait()

    def found(j, column):
        entry = tab[j, column]
        return entry, jnp.bitwise_and(lax.shift_right_logical(jnp.maximum(entry - 1, 0), 7), TILES - 1)

    def pack(i, dx, j, _):
        for k in range(2):
            entry, t = found(2 * j + k, NX + dx % NX)
            part = adj[t, q_rows(0), :]
            send[i, j, :, k * B : (k + 1) * B] = jnp.where(entry > 0, part, jnp.zeros_like(part))
        return 0

    def keep(j, _):
        for k in range(2):
            entry, t = found(2 * j + k, NX)
            part = adj[t]
            tiles[0, j, :, k * B : (k + 1) * B] = jnp.where(entry > 0, part, jnp.zeros_like(part))
        return 0

    def quarter(i, dy, lo=0, n=PAIRS):
        return tiles.at[i, pl.ds(lo, n), q_rows(dy), :]

    hops_x = (1, -1, 2)
    for i, dx in enumerate(hops_x):
        lax.fori_loop(0, PAIRS, functools.partial(pack, i, dx), 0)
        go(remote(send.at[i], quarter(-dx % NX, 0), xs.at[i], xr.at[i], me.at(dx=dx)))

    half = (PAIRS + 1) // 2
    cut = ((0, half), (half, PAIRS - half))

    def tiles_from_x(i):
        dx = hops_x[i]
        spot = quarter(-dx % NX, 0)
        remote(spot, spot, xs.at[i], xr.at[i], me.at(dx=-dx)).wait_recv()
        for way, d in WAYS:
            go(remote(spot, spot, ys.at[i * 4 + way], yr.at[i * 4 + way], me.at(dy=d)))

    def tiles_from_y(i):
        for way, d in WAYS:
            spot = quarter(-hops_x[i] % NX, -d)
            sem = i * 4 + way
            remote(spot, spot, ys.at[sem], yr.at[sem], me.at(dy=-d)).wait_recv()
            part = quarter(-hops_x[i] % NX, -d, *cut[way])
            go(remote(part, part, ys.at[sem + 2], yr.at[sem + 2], me.at(dy=d)))

    def tiles_last(i):
        for way, d in WAYS:
            spot = quarter(-hops_x[i] % NX, 2, *cut[way])
            sem = i * 4 + way + 2
            remote(spot, spot, ys.at[sem], yr.at[sem], me.at(dy=-d)).wait_recv()

    def place_of(hops, side):
        z = lax.rem(me.z + (NZ - hops), NZ)
        return z * NC + (1 - me.c if side else me.c)

    def spread(i, rd, pair):
        rows = []
        for k in range(2):
            entry = jnp.maximum(tab[2 * pair + k, rd] - 1, 0)
            tile = tiles[rd, pair, :, k * B : (k + 1) * B]
            at = pl.ds((2 * i + k) * B, B)
            r = lax.shift_right_logical(entry, 11)
            for row in range(R):
                lhs[row * B : (row + 1) * B, at] = jnp.where(r == row, tile, jnp.zeros_like(tile))
            rows.append((jnp.bitwise_and(entry, 127), at))
        return rows

    def product(layer, step, rd):
        held = blocks[layer]
        for i, (hops, side) in enumerate(STEPS[step]):
            for entry, at in spread(i, rd, place_of(hops, side)):
                rhs[at, :] = held[hops][side][jnp.bitwise_and(entry, 7)]
        n = len(STEPS[step])
        if step == 4:
            for entry, at in spread(n, rd, PAIRS - 1):
                b, q = jnp.bitwise_and(entry, 7), lax.shift_right_logical(entry, 3)
                got = held[0][0][b]
                for hops in range(NZ):
                    for side in range(2):
                        if hops or side:
                            got = jnp.where(q == place_of(hops, side), held[hops][side][b], got)
                rhs[at, :] = got
            n += 1
        width = n * 2 * B
        total = jnp.dot(lhs[:, :width], rhs[:width, :], preferred_element_type=F32)
        acc[rd] = total if step == 0 else acc[rd] + total

    def layer_end(layer, weight, last, put):
        part, relay_in, relay_out, sums_in, agg, xs, xr, ys, yr = ends[layer]
        halves = lambda k: (pl.ds(k * RC, HC), pl.ds(k * RC + HC, HC))

        def x_far(k):
            rows = pl.ds(k * RC, RC)
            part[2, rows, :] = acc[2, rows, :].astype(BF)
            for way, d in WAYS:
                i = (way * NE + k) * 3
                go(remote(part.at[2, halves(k)[way]], relay_in.at[way, k], xs.at[i], xr.at[i], me.at(dx=d)))

        def x_near(k):
            for way, d in WAYS:
                i = (way * NE + k) * 3 + 1
                rows = halves(k)[1 - way]
                part[d % NX, rows, :] = acc[d % NX, rows, :].astype(BF)
                go(remote(part.at[d % NX, rows], sums_in.at[way, rows], xs.at[i], xr.at[i], me.at(dx=d)))

        def x_relay(k):
            for way, d in WAYS:
                i = (way * NE + k) * 3
                spot = relay_in.at[way, k]
                remote(spot, spot, xs.at[i], xr.at[i], me.at(dx=-d)).wait_recv()
                rows = halves(k)[way]
                relay_out[way, k] = (acc[d % NX, rows, :] + relay_in[way, k].astype(F32)).astype(BF)
                go(remote(relay_out.at[way, k], sums_in.at[way, rows], xs.at[i + 2], xr.at[i + 2], me.at(dx=d)))

        def x_sum(k):
            for way, d in WAYS:
                for j, rows in ((1, halves(k)[1 - way]), (2, halves(k)[way])):
                    i = (way * NE + k) * 3 + j
                    spot = sums_in.at[way, rows]
                    remote(spot, spot, xs.at[i], xr.at[i], me.at(dx=-d)).wait_recv()
            rows = pl.ds(k * RC, RC)
            total = acc[0, rows, :] + sums_in[0, rows, :].astype(F32) + sums_in[1, rows, :].astype(F32)
            agg[me.y, rows, :] = total.astype(BF)
            for way, d in WAYS:
                i = (way * NE + k) * 2
                spot = agg.at[me.y, rows]
                go(remote(spot, spot, ys.at[i], yr.at[i], me.at(dy=d)))

        def y_pass(k):
            for way, d in WAYS:
                i = (way * NE + k) * 2
                spot = agg.at[me.y_of(-d), pl.ds(k * RC, RC)]
                remote(spot, spot, ys.at[i], yr.at[i], me.at(dy=-d)).wait_recv()
                spot = agg.at[me.y_of(-d), halves(k)[way]]
                go(remote(spot, spot, ys.at[i + 1], yr.at[i + 1], me.at(dy=d)))

        def transform(k):
            for way, d in WAYS:
                i = (way * NE + k) * 2 + 1
                spot = agg.at[me.y_of(2), halves(k)[way]]
                remote(spot, spot, ys.at[i], yr.at[i], me.at(dy=-d)).wait_recv()
            total = jnp.zeros((RC, COLS), F32)
            for y in range(NY):
                total += jnp.dot(
                    agg[y, pl.ds(k * RC, RC), :], weight[pl.ds(y * COLS, COLS), :], preferred_element_type=F32
                )
            put(k, total)

        def finish():
            for turn in range(NE + 3):
                if turn < NE:
                    x_relay(turn)
                if turn + 1 < NE:
                    x_near(turn + 1)
                rest(turn)

        def rest(turn):
            if 0 <= turn - 1 < NE:
                x_sum(turn - 1)
            if 0 <= turn - 2 < NE:
                y_pass(turn - 2)
            if 0 <= turn - 3 < NE:
                transform(turn - 3)

        last(2)
        for k in range(NE):
            x_far(k)
        lax.fori_loop(0, 2, lambda i, _: last(2 * i + 1) or 0, 0)
        x_near(0)
        last(0)
        finish()

    first = rings[0]
    both = lambda s, k: [first.arrive(way, s, k, s < 2 or (s == 2 and (k < NP // 2) == (way == 0))) for way in range(2)]
    lax.fori_loop(0, PAIRS, keep, 0)
    tile_turns = [
        lambda: (tiles_from_x(0), tiles_from_x(1)),
        lambda: tiles_from_x(2),
        lambda: tiles_from_y(0),
        lambda: tiles_from_y(1),
        lambda: tiles_from_y(2),
    ]
    for i in range(6):
        for k in range(NP // 2):
            both(i // 2, i % 2 * (NP // 2) + k)
        if i % 2:
            first.share(i // 2)
        if i < len(tile_turns):
            tile_turns[i]()
    for i in range(3):
        tiles_last(i)
    loads[1].wait()

    def products(*steps):
        def one(rd, _):
            for step in steps:
                product(0, step, rd)
            return 0

        lax.fori_loop(0, NX, one, 0)

    first.from_sibling(0, 1, 7)
    products(0, 1)
    first.from_sibling(2, 6)
    products(2)
    for k in range(NP):
        first.arrive(0 if k < NP // 2 else 1, 3, k, False)
    first.share(3)
    first.from_sibling(3, 5)
    loads[2].wait()
    loads[3].wait()
    second = rings[1]

    per = R // NE

    def put_hidden(k, total):
        hidden = jnp.maximum(total, 0.0).astype(BF).reshape(per, B, COLS)
        blocks[1][0][0][pl.ds(k * per, per)] = hidden
        if (k + 1) * per % PER == 0:
            second.send_own((k + 1) * per // PER - 1)

    def last_products(layer):
        def last(rd):
            product(layer, 3, rd)
            if isinstance(rd, int) and rd == 2:
                rings[layer].from_sibling(4, 8)
            product(layer, 4, rd)

        return last

    layer_end(0, w1, last_products(0), put_hidden)

    second.run(lambda step, k: product(1, step, k))

    def put_out(k, total):
        done[pl.ds(k * per, per)] = total.astype(BF).reshape(per, B, COLS)

    layer_end(1, w2, last_products(1), put_out)

    slots = [mig[m, me.dom] for m in range(2)]
    for m in range(2):
        leave[m] = done[slots[m]]
    move = remote(leave, came, ms, mr, me.along(1))
    move.start()
    move.wait()
    done[pl.ds(R, 2)] = came[...]
    for r in range(R):
        at = jnp.where(slots[0] == r, R, jnp.where(slots[1] == r, R + 1, r))
        out[pl.ds(r * B, B), :] = done[at]
    for ring in rings:
        ring.finish()
    for copy in started:
        copy.wait_send()


def run_all(sources, mig_slot, features, adjacency, weight_one, weight_two):
    vmem = pl.BlockSpec(memory_space=pltpu.VMEM)
    smem = pl.BlockSpec(memory_space=pltpu.SMEM)
    hbm = pl.BlockSpec(memory_space=pl.ANY)
    dma = pltpu.SemaphoreType.DMA
    return pl.pallas_call(
        whole_kernel,
        name="two_layers",
        out_shape=jax.ShapeDtypeStruct((ROWS, COLS), BF),
        in_specs=[vmem, smem, hbm, hbm, hbm, hbm],
        out_specs=vmem,
        scratch_shapes=[pltpu.VMEM((R, B, COLS), BF)] * (4 * NZ)
        + [
            pltpu.VMEM((TILES, B, B), BF),
            pltpu.VMEM((NX, PAIRS, B, 2 * B), BF),
            pltpu.VMEM((3, PAIRS, QROWS, 2 * B), BF),
            pltpu.VMEM((NY * COLS, COLS), BF),
            pltpu.VMEM((NY * COLS, COLS), BF),
            pltpu.VMEM((NX, ROWS, COLS), F32),
            pltpu.VMEM((ROWS, 8 * B), BF),
            pltpu.VMEM((8 * B, COLS), BF),
            pltpu.VMEM((R + 2, B, COLS), BF),
            pltpu.VMEM((2, B, COLS), BF),
            pltpu.VMEM((2, B, COLS), BF),
            dma((5,)),
            dma((3,)),
            dma((3,)),
            dma((12,)),
            dma((12,)),
            dma,
            dma,
            pltpu.VMEM((40, 128), jnp.int32),
            pltpu.SMEM((40, 128), jnp.int32),
        ]
        + ring_scratch() * 2
        + end_scratch() * 2,
        compiler_params=pltpu.CompilerParams(
            collective_id=0, has_side_effects=True, vmem_limit_bytes=60 * 1024 * 1024
        ),
    )(sources, mig_slot.T, features, adjacency, weight_one, weight_two)


def on_device(features, adjacency, tile_src, mig_slot, weight_one, weight_two):
    dom = lax.axis_index("dom")
    z, c = lax.rem(lax.div(dom, NC), NZ), lax.rem(dom, NC)
    grid = tile_src.reshape(NX, NZ, NC, TILES)
    sources = lax.dynamic_slice(grid, (0, z, c, 0), (NX, 1, 1, TILES)).reshape(NX, TILES)
    return run_all(
        sources, mig_slot, features.reshape(R, B, COLS), adjacency.reshape(TILES, B, B), weight_one, weight_two
    )


def solution(mesh):
    in_specs = (P("dom", "feat"), P("dom", None, None, None), P(), P(), P(), P())
    return jax.shard_map(
        on_device, mesh=mesh, in_specs=in_specs, out_specs=P("dom", "feat"), check_vma=False
    )
```
